128 devices in a mesh: grp: 8 (over x, core), sub: 16 (over y, z).
Axes of the slice: x: 4, y: 4, z: 4, core: 2. Of those that a mesh axis runs over, the one named last changes fastest.
Arguments:
- currents: bfloat16 [128, 1048576], P(None, ('grp', 'sub')), may hold values from -6 to 6
- leaf_segment_count: int32 [128, 64], P(('grp', 'sub')), may hold values from 1 to 128, 6144 in all within a row
- leaf_basis: bfloat16 [8192, 128, 64], P(('grp', 'sub')), may hold values from -0.5 to 0.5
- transfers: bfloat16 [16128, 64, 64], P(('grp', 'sub')), may hold values from -0.625 to 0.625
- coupling: bfloat16 [16256, 6, 64, 64], P(('grp', 'sub')), may hold values from -0.3125 to 0.3125
- far_sources: int32 [16256, 6], P(('grp', 'sub')), may hold values from 0 to 8191, as said below
- near_tiles: bfloat16 [8192, 5, 128, 128], P(('grp', 'sub')), may hold values from -0.25 to 0.25
- near_sources: int32 [8192, 5], P(('grp', 'sub')), may hold values from 0 to 8191, as said below
Outputs:
- voltages: float32 [128, 1048576], P(None, ('grp', 'sub'))
The draws below stay inside these ranges and needn't reach their ends.
Inputs may be any that keep to these rules, and one draw needn't show every extreme that they name: `far_sources`: the sources of a target at levels 0 and 1 lie in its group and differ from it by at most 8 in cluster index; at levels 2 to 5 they lie in its group; at level 6 they are any of the 128 clusters. `near_sources`: Near-field sources of a leaf lie in its group and differ from it by at most 2 in leaf index; slot 0 is the leaf itself.
All inputs are finite; a program needn't handle non-finite values.
Results may differ from the reference program's by a relative error of at most 0.024.
Values may be sent and summed in bfloat16 or wider, within the bound.
A program may use at most 192 MiB of HBM per device.

```python
import math
import jax
import jax.numpy as jnp
import numpy as np
from jax import lax

LEVELS = 6
LEAF_DEV = 64
LEAF_SIZE = 128
K = 64
NC = 128
FAR = 6
NEAR = 5
REACH = 8
NEAR_REACH = 2
TARG_DEV = 127
TRANS_DEV = 126
TOTAL_LEAVES = 8192
GROUP_LEAVES = 1024
SEGS = 1048576
N_SUB = 16
DEVICES = 128


def draw_near_sources(key, part):
    key = jax.random.fold_in(key, 11)
    leaf = jnp.arange(TOTAL_LEAVES, dtype=jnp.int32)[:, None]
    offsets = jax.random.randint(key, (TOTAL_LEAVES, NEAR), -NEAR_REACH, NEAR_REACH + 1).astype(jnp.int32)
    slot_position = jnp.arange(NEAR, dtype=jnp.int32)[None, :]
    offsets = jnp.where(slot_position == 0, 0, jnp.where(slot_position == 1, NEAR_REACH, jnp.where(slot_position == 2, -NEAR_REACH, offsets)))
    lowest = leaf // GROUP_LEAVES * GROUP_LEAVES
    return jnp.clip(leaf + offsets, lowest, lowest + GROUP_LEAVES - 1).astype(jnp.int32)


def draw_far_sources(key, part):
    key = jax.random.fold_in(key, 23)
    level_lookup_table = np.concatenate([np.full(LEAF_DEV // 2 ** lv, lv) for lv in range(LEVELS + 1)]).astype(np.int32)
    local_lookup_table = np.concatenate([np.arange(LEAF_DEV // 2 ** lv) for lv in range(LEVELS + 1)]).astype(np.int32)
    rows = DEVICES * TARG_DEV
    device_index = jnp.arange(rows, dtype=jnp.int32) // TARG_DEV
    level = jnp.tile(jnp.asarray(level_lookup_table), DEVICES)
    local = jnp.tile(jnp.asarray(local_lookup_table), DEVICES)
    count = jnp.right_shift(jnp.int32(LEAF_DEV), level)
    target = device_index * count + local
    group_size = N_SUB * count
    group_low = device_index // N_SUB * group_size
    key_near, key_wide = jax.random.split(key)
    offsets = jax.random.randint(key_near, (rows, FAR), -REACH, REACH + 1).astype(jnp.int32)
    slot_position = jnp.arange(FAR, dtype=jnp.int32)[None, :]
    offsets = jnp.where(slot_position == 0, REACH, jnp.where(slot_position == 1, -REACH, offsets))
    close_pick = jnp.clip(target[:, None] + offsets, group_low[:, None], group_low[:, None] + group_size[:, None] - 1)
    raw = jax.random.randint(key_wide, (rows, FAR), 0, 1 << 30).astype(jnp.int32)
    group_pick = group_low[:, None] + raw % group_size[:, None]
    root_pick = raw % DEVICES
    level_col = level[:, None]
    selected_rows = jnp.where(level_col <= 1, close_pick, jnp.where(level_col < LEVELS, group_pick, root_pick))
    return selected_rows.astype(jnp.int32)


def levels(stream_key, extent, cuts, smallest, top_value):
    level = 1.0
    for position, parts in cuts:
        draws = jax.random.uniform(jax.random.fold_in(jax.random.fold_in(stream_key, 6), position), (parts,), jnp.float32, smallest / len(cuts), top_value / len(cuts))
        level = level * jnp.repeat(jnp.exp(draws), extent[position] // parts).reshape((-1,) + (1,) * (len(extent) - 1 - position))
    return level


def split_up(count, total, bound, skew):
    loads = [(1 << 20) // math.isqrt(rank ** skew) + 1 for rank in range(2, count + 1)]
    surplus, counts = total - bound - (count - 1), [1] * (count - 1)
    while surplus > 0:
        free = [i for i in range(count - 1) if counts[i] < bound]
        whole, remaining = sum([loads[i] for i in free]), surplus
        for i in free:
            addition = min(bound - counts[i], max(1, remaining * loads[i] // whole), surplus)
            counts[i] = counts[i] + addition
            surplus = surplus - addition
    return np.array([bound] + counts)


def ragged(rng, count, total, limit, slope):
    if count == 2:
        one = jax.random.randint(rng, (), max(1, total - limit), min(limit, total - 1) + 1)
        return jnp.stack([one, total - one])
    tallies = jnp.asarray(split_up(count, total, limit, slope), jnp.int32)
    couples = (count - 1) // 2
    giver, receiver = tallies[1:1 + 2 * couples:2], tallies[2:2 + 2 * couples:2]
    margin = jnp.minimum(giver - 1, limit - receiver)
    passed = jax.random.randint(jax.random.fold_in(rng, 1), (couples,), 0, 1 << 20) % (margin + 1)
    tallies = tallies.at[1:1 + 2 * couples:2].set(giver - passed).at[2:2 + 2 * couples:2].set(receiver + passed)
    return tallies[jax.random.permutation(jax.random.fold_in(rng, 2), count)]


def bell_draw(stream_key, dims, scale, reach, shards=(), kind=jnp.bfloat16):
    drawn = scale * jax.random.normal(stream_key, dims, jnp.float32)
    if shards:
        drawn = drawn * levels(stream_key, dims, shards, -0.22, 0.18)
    return jnp.clip(drawn, -reach, reach).astype(kind)


def setup_inputs(seed: int = 0) -> dict:
    arg_keys = jax.random.split(jax.random.key(seed), 9)
    return {
        "currents": bell_draw(arg_keys[0], (NC, SEGS), 1.0, 6.0, ((1, 128),)),
        "leaf_segment_count": jax.vmap(lambda own: ragged(own, LEAF_DEV, LEAF_SIZE * LEAF_DEV * 3 // 4, LEAF_SIZE, 2))(jax.random.split(arg_keys[1], DEVICES)).reshape((DEVICES, LEAF_DEV)).astype(jnp.int32),
        "leaf_basis": bell_draw(arg_keys[2], (TOTAL_LEAVES, LEAF_SIZE, K), LEAF_SIZE ** -0.5, 0.5, ((0, 128),)),
        "transfers": bell_draw(arg_keys[3], (DEVICES * TRANS_DEV, K, K), (3 * K // 2) ** -0.5, 0.625, ((0, 128),)),
        "coupling": bell_draw(arg_keys[4], (DEVICES * TARG_DEV, FAR, K, K), (FAR * K) ** -0.5, 0.3125, ((0, 128),)),
        "far_sources": draw_far_sources(jax.random.fold_in(arg_keys[8], 71), 0),
        "near_tiles": bell_draw(arg_keys[6], (TOTAL_LEAVES, NEAR, LEAF_SIZE, LEAF_SIZE), (NEAR * LEAF_SIZE) ** -0.5, 0.25, ((0, 128),)),
        "near_sources": draw_near_sources(jax.random.fold_in(arg_keys[8], 71), 0),
    }


def level_rows(matrices, level):
    count = LEAF_DEV // (2 ** level)
    start = 2 * LEAF_DEV - 2 * count
    return matrices[:, start:start + count]


def reference(currents, leaf_segment_count, leaf_basis, transfers, coupling, far_sources, near_tiles, near_sources):
    leaf_clusters = DEVICES * LEAF_DEV
    slots = jnp.arange(LEAF_SIZE, dtype=jnp.int32)[None, :]
    live = (slots < leaf_segment_count.reshape(leaf_clusters, 1)).astype(currents.dtype)
    masked = currents.reshape(NC, leaf_clusters, LEAF_SIZE) * live[None]
    basis = leaf_basis.astype(jnp.float32)
    coeffs = [jnp.einsum("lsk,nls->nlk", basis, masked.astype(jnp.float32)).astype(jnp.bfloat16)]
    trans = transfers.reshape(DEVICES, TRANS_DEV, K, K)
    couple = coupling.reshape(DEVICES, TARG_DEV, FAR, K, K)
    sources = far_sources.reshape(DEVICES, TARG_DEV, FAR)

    def child_mats(level):
        block = level_rows(trans, level)
        return block.reshape(-1, K, K).astype(jnp.float32)

    for level in range(1, LEVELS + 1):
        mapped = jnp.einsum("ckj,nck->ncj", child_mats(level - 1), coeffs[-1].astype(jnp.float32))
        coeffs.append(mapped.reshape(NC, -1, 2, K).sum(axis=2).astype(jnp.bfloat16))

    fields = []
    for level in range(LEVELS + 1):
        level_coeff = coeffs[level]

        def one_device(args):
            block_matrices, ids = args
            selected_rows = jnp.take(level_coeff, ids, axis=1).astype(jnp.float32)
            return jnp.einsum("cjab,ncjb->nca", block_matrices.astype(jnp.float32), selected_rows)

        result = lax.map(one_device, (level_rows(couple, level), level_rows(sources, level)))
        fields.append(jnp.transpose(result, (1, 0, 2, 3)).reshape(NC, -1, K))

    down = fields[LEVELS]
    for level in range(LEVELS, 0, -1):
        parent = jnp.repeat(down.astype(jnp.bfloat16), 2, axis=1).astype(jnp.float32)
        down = fields[level - 1] + jnp.einsum("ckj,ncj->nck", child_mats(level - 1), parent)
    smooth = jnp.einsum("lsk,nlk->nls", basis, down.astype(jnp.bfloat16).astype(jnp.float32))

    tiles = near_tiles.reshape(DEVICES, LEAF_DEV, NEAR, LEAF_SIZE, LEAF_SIZE)
    near_ids = near_sources.reshape(DEVICES, LEAF_DEV, NEAR)

    def near_device(args):
        block_matrices, ids = args
        selected_rows = jnp.take(masked, ids, axis=1).astype(jnp.float32)
        return jnp.einsum("tjab,ntjb->nta", block_matrices.astype(jnp.float32), selected_rows)

    nearby = lax.map(near_device, (tiles, near_ids))
    nearby = jnp.transpose(nearby, (1, 0, 2, 3)).reshape(NC, leaf_clusters, LEAF_SIZE)
    voltages = (smooth + nearby) * live[None].astype(jnp.float32)
    return voltages.reshape(NC, SEGS)
```

```python
import functools

import jax
import jax.numpy as jnp
from jax import lax
from jax.experimental import pallas as pl
from jax.experimental.pallas import tpu as pltpu
from jax.sharding import PartitionSpec as P

LEVELS = 6
REACH = 8
NEAR_REACH = 2
SIDE = 4
SUBS = 16
XS = 4
F32 = jnp.float32
BF16 = jnp.bfloat16
VMEM_LIMIT = 60 * 1024 * 1024

C_ROWS = 127 * 64
NT = (((1,), (1,)), ((), ()))
TN = (((0,), (0,)), ((), ()))


def span(level):
    count = 64 >> level
    return 128 - 2 * count, count


def up_kernel(cnt, cur, bas, tr, masked, c0, c1, c2, c35, c6, e_out, e32):
    def relayout(k, carry):
        slab = jnp.concatenate([tr[k], tr[k + 32]], axis=0).astype(F32)
        e32[pl.ds(k, 126, stride=32), :] = slab.T
        return carry

    lax.fori_loop(0, 32, relayout, 0, unroll=4)

    def matrices(t, count):
        rows = e32[pl.ds(pl.multiple_of(t * 32, 32), 32 * count), :].astype(BF16)
        parts = []
        for c in range(count):
            part = rows[32 * c : 32 * (c + 1)]
            parts += [part[:, :64], part[:, 64:]]
        return jnp.concatenate(parts, axis=0)

    lane = lax.broadcasted_iota(jnp.int32, (1, 128), 1)

    def leaf(l, carry):
        live = (lane < cnt[0, l]).astype(F32).astype(BF16)
        m = cur[:, pl.ds(pl.multiple_of(l * 128, 128), 128)] * live
        masked[l] = m
        c0[l] = lax.dot_general(bas[l], m, NT, preferred_element_type=F32).astype(BF16)
        return carry

    lax.fori_loop(0, 64, leaf, 0, unroll=4)

    def lift(level, src, src_at, dst, dst_at):
        start, _ = span(level - 1)
        _, count = span(level)

        def parent(p, carry):
            e = matrices(start + 2 * p, 2)
            pair = src[pl.ds(src_at + 2 * p, 2)].reshape(128, 128)
            dst[dst_at + p] = lax.dot_general(e, pair, TN, preferred_element_type=F32).astype(BF16)
            return carry

        lax.fori_loop(0, count, parent, 0, unroll=min(count, 4))

    lift(1, c0, 0, c1, 0)
    lift(2, c1, 0, c2, 0)
    lift(3, c2, 0, c35, 0)
    lift(4, c35, 0, c35, 8)
    lift(5, c35, 8, c35, 12)
    lift(6, c35, 12, c6, 0)

    def keep(t, carry):
        e_out[t] = matrices(t, 1)
        return carry

    lax.fori_loop(0, 126, keep, 0, unroll=2)


def up_pass(cnt, cur, bas, tr):
    vm = pl.BlockSpec(memory_space=pltpu.VMEM)
    return pl.pallas_call(
        up_kernel,
        out_shape=(
            jax.ShapeDtypeStruct((64, 128, 128), BF16),
            jax.ShapeDtypeStruct((64, 64, 128), BF16),
            jax.ShapeDtypeStruct((32, 64, 128), BF16),
            jax.ShapeDtypeStruct((16, 64, 128), BF16),
            jax.ShapeDtypeStruct((14, 64, 128), BF16),
            jax.ShapeDtypeStruct((1, 64, 128), BF16),
            jax.ShapeDtypeStruct((126, 64, 64), BF16),
        ),
        in_specs=[pl.BlockSpec(memory_space=pltpu.SMEM), vm, vm, vm],
        out_specs=(vm,) * 7,
        scratch_shapes=[pltpu.VMEM((126 * 32, 128), F32)],
        compiler_params=pltpu.CompilerParams(vmem_limit_bytes=VMEM_LIMIT),
        name="up_pass",
    )(cnt, cur, bas, tr)


STEPS = (
    (None, 0, 0, 0, 0, 1),
    (None, 0, 0, 0, 0, -1),
    (None, 0, 0, 0, 1, 1),
    (None, 0, 0, 0, 1, -1),
    (0, -1, 0, 1, 0, 1),
    (0, -1, 0, 0, 1, 1),
    (0, -1, 0, 0, 1, -1),
    (1, 1, 0, 2, 0, -1),
    (1, 1, 0, 0, 1, 1),
    (1, 1, 0, 0, 1, -1),
    (2, 0, -1, 1, 1, 1),
    (3, 0, 1, 2, 1, -1),
    (4, 2, 0, 1, 1, 1),
    (4, 2, 0, 1, 1, -1),
    (7, 2, 0, 2, 1, 1),
    (7, 2, 0, 2, 1, -1),
    (8, 1, -1, 0, 1, 1),
    (6, -1, 1, 0, 1, -1),
    (12, 2, -1, 1, 1, 1),
    (15, 2, 1, 2, 1, -1),
)
N_STEPS = len(STEPS)
WAVES = ((0, 1, 2, 3), (4, 7, 8, 6), (12, 15), (5, 9, 10, 11, 13, 14, 16, 17, 18, 19))


def field_kernel(
    masked, c0, c1, c2, c35, c6, coupling, near_tiles, far, near,
    fields, nearby,
    xm, x0, x1, g2, g35, roots, cin, c32, tiles,
    halo_send, halo_recv, send2, recv2, send35, recv35,
    root_send, root_recv, xs_send, xs_recv, core_send, core_recv, local_sem, tile_sem,
):
    grp = lax.axis_index("grp")
    sub = lax.axis_index("sub")
    y = sub // SIDE
    z = sub % SIDE
    core = grp % 2
    x = grp // 2

    def at(dy, dz):
        return ((y + dy + SIDE) % SIDE) * SIDE + (z + dz + SIDE) % SIDE

    def along_x(d):
        return ((x + d) % XS) * 2 + core

    other_core = x * 2 + (1 - core)

    cin_copy = pltpu.make_async_copy(coupling, cin, local_sem.at[0])
    cin_copy.start()
    tiles_copy = pltpu.make_async_copy(near_tiles, tiles, tile_sem.at[0])

    own = (
        pltpu.make_async_copy(masked, xm.at[pl.ds(NEAR_REACH, 64)], local_sem.at[1]),
        pltpu.make_async_copy(c0, x0.at[pl.ds(REACH, 64)], local_sem.at[2]),
        pltpu.make_async_copy(c1, x1.at[pl.ds(REACH, 32)], local_sem.at[3]),
        pltpu.make_async_copy(c2, g2.at[pl.ds(sub * 16, 16)], local_sem.at[4]),
        pltpu.make_async_copy(c35, g35.at[pl.ds(sub * 14, 14)], local_sem.at[5]),
        pltpu.make_async_copy(c6, roots.at[pl.ds(grp * SUBS + sub, 1)], local_sem.at[6]),
    )
    for copy in own:
        copy.start()
    tiles_copy.start()

    barrier = pltpu.get_barrier_semaphore()
    for i in range(1, SUBS):
        pl.semaphore_signal(
            barrier, inc=1, device_id=(grp, (sub + i) % SUBS), device_id_type=pl.DeviceIdType.MESH
        )
    for d in range(1, XS):
        pl.semaphore_signal(
            barrier, inc=1, device_id=(along_x(d), sub), device_id_type=pl.DeviceIdType.MESH
        )
    pl.semaphore_signal(
        barrier, inc=1, device_id=(other_core, sub), device_id_type=pl.DeviceIdType.MESH
    )
    pl.semaphore_wait(barrier, SUBS - 1 + XS - 1 + 1)

    def remote(src, dst, send, recv, device):
        return pltpu.make_async_remote_copy(
            src_ref=src, dst_ref=dst, send_sem=send, recv_sem=recv,
            device_id=device, device_id_type=pl.DeviceIdType.MESH,
        )

    mine = grp * SUBS + sub
    root_copies = [
        remote(c6, roots.at[pl.ds(mine, 1)], root_send.at[i - 1], root_recv.at[i - 1],
               (grp, (sub + i) % SUBS))
        for i in range(1, SUBS)
    ]
    for copy in root_copies:
        copy.start()

    up, down = (grp, (sub + 1) % SUBS), (grp, (sub + SUBS - 1) % SUBS)
    halos = []
    for i, (src, dst, width, count) in enumerate(
        ((masked, xm, NEAR_REACH, 64), (c0, x0, REACH, 64), (c1, x1, REACH, 32))
    ):
        halos.append(
            remote(src.at[pl.ds(count - width, width)], dst.at[pl.ds(0, width)],
                   halo_send.at[2 * i], halo_recv.at[2 * i], up)
        )
        halos.append(
            remote(src.at[pl.ds(0, width)], dst.at[pl.ds(count + width, width)],
                   halo_send.at[2 * i + 1], halo_recv.at[2 * i + 1], down)
        )
    for copy in halos:
        copy.start()

    def step_copy(tree, i):
        src, dst, n, z_first, send, recv = tree
        _, first, second, part, dim, way = STEPS[i]
        offset = (second, first) if z_first else (first, second)
        move = (way, 0) if (dim == 1) == z_first else (0, way)
        slot = at(*offset)
        half = n // 2
        low, width = ((0, n), (0, half), (half, n - half))[part]
        rows = pl.ds(slot * n + low, width)
        source = src if (first, second) == (0, 0) else dst.at[rows]
        return remote(source, dst.at[rows], send.at[i], recv.at[i], (grp, at(*move)))

    trees = (
        (c2, g2, 16, True, send2, recv2),
        (c35, g35, 14, False, send35, recv35),
    )
    copies = [[step_copy(tree, i) for i in range(N_STEPS)] for tree in trees]
    for i in range(4):
        for c in copies:
            c[i].start()

    def wave(k):
        for i in WAVES[k]:
            for c in copies:
                c[i].wait_recv()
            for j in range(N_STEPS):
                if STEPS[j][0] == i:
                    for c in copies:
                        c[j].start()

    def relayout(low, high):
        def one(a, carry):
            for qp in range(3):
                slab = cin[pl.ds(2 * qp, 2), a].reshape(128, 127).astype(F32)
                c32[pl.ds(qp * C_ROWS + a, 127, stride=64), :] = slab.T
            return carry

        lax.fori_loop(low, high, one, 0, unroll=2)

    cin_copy.wait()
    relayout(0, 16)
    wave(0)
    relayout(16, 32)

    for copy in root_copies:
        copy.wait_recv()
    own[5].wait()
    block = roots.at[pl.ds(grp * SUBS, SUBS)]
    x_copies = [
        remote(block, block, xs_send.at[d - 1], xs_recv.at[d - 1], (along_x(d), sub))
        for d in range(1, XS)
    ]
    for copy in x_copies:
        copy.start()
    core_copies = []
    for d in range(XS):
        held = roots.at[pl.ds(along_x(d) * SUBS, SUBS)]
        core_copies.append(
            remote(held, held, core_send.at[d], core_recv.at[d], (other_core, sub))
        )
    core_copies[0].start()

    wave(1)
    relayout(32, 64)
    wave(2)
    for copy in x_copies:
        copy.wait_recv()
    for copy in core_copies[1:]:
        copy.start()

    own[0].wait()
    halos[0].wait_recv()
    halos[1].wait_recv()
    tiles_copy.wait()
    device_index = grp * SUBS + sub
    near_base = device_index * 64 - NEAR_REACH

    def near_leaf(t, carry):
        total = None
        for q in range(5):
            source = xm[jnp.clip(near[q, t] - near_base, 0, 64 + 2 * NEAR_REACH - 1)]
            part = lax.dot_general(source, tiles[t, q], NT, preferred_element_type=F32)
            total = part if total is None else total + part
        nearby[t] = total.astype(nearby.dtype)
        return carry

    lax.fori_loop(0, 64, near_leaf, 0, unroll=2)

    def couple(level, buffer, place):
        start, count = span(level)

        def target(i, carry):
            t = start + i
            matrix = jnp.concatenate(
                [
                    c32[pl.ds(pl.multiple_of(qp * C_ROWS + t * 64, 64), 64), :].astype(BF16)
                    for qp in range(3)
                ],
                axis=1,
            )
            last = buffer.shape[0] - 1
            stacked = jnp.concatenate(
                [buffer[jnp.clip(place(far[q, t]), 0, last)] for q in range(6)], axis=0
            )
            fields[t] = jnp.dot(matrix, stacked, preferred_element_type=F32)
            return carry

        lax.fori_loop(0, count, target, 0, unroll=min(count, 2))

    own[1].wait()
    halos[2].wait_recv()
    halos[3].wait_recv()
    couple(0, x0, lambda s: s - (device_index * 64 - REACH))
    own[2].wait()
    halos[4].wait_recv()
    halos[5].wait_recv()
    couple(1, x1, lambda s: s - (device_index * 32 - REACH))

    wave(3)
    own[3].wait()
    own[4].wait()
    couple(2, g2, lambda s: s - grp * SUBS * 16)

    def place35(level, offset):
        _, count = span(level)

        def place(s):
            relative = s - grp * SUBS * count
            return (relative // count) * 14 + offset + relative % count

        return place

    couple(3, g35, place35(3, 0))
    couple(4, g35, place35(4, 8))
    couple(5, g35, place35(5, 12))
    for copy in core_copies:
        copy.wait_recv()
    couple(6, roots, lambda s: s)

    for copy in root_copies + halos + x_copies + core_copies + copies[0] + copies[1]:
        copy.wait_send()


def comm_fields(masked, c0, c1, c2, c35, c6, coupling, near_tiles, far, near):
    vm = pl.BlockSpec(memory_space=pltpu.VMEM)
    hbm = pl.BlockSpec(memory_space=pl.ANY)
    sm = pl.BlockSpec(memory_space=pltpu.SMEM)
    dma = pltpu.SemaphoreType.DMA
    return pl.pallas_call(
        field_kernel,
        out_shape=(
            jax.ShapeDtypeStruct((127, 64, 128), F32),
            jax.ShapeDtypeStruct((64, 128, 128), BF16),
        ),
        in_specs=[hbm] * 8 + [sm, sm],
        out_specs=(vm, vm),
        scratch_shapes=[
            pltpu.VMEM((64 + 2 * NEAR_REACH, 128, 128), BF16),
            pltpu.VMEM((64 + 2 * REACH, 64, 128), BF16),
            pltpu.VMEM((32 + 2 * REACH, 64, 128), BF16),
            pltpu.VMEM((256, 64, 128), BF16),
            pltpu.VMEM((224, 64, 128), BF16),
            pltpu.VMEM((128, 64, 128), BF16),
            pltpu.VMEM((6, 64, 64, 127), BF16),
            pltpu.VMEM((3 * C_ROWS, 128), F32),
            pltpu.VMEM((64, 5, 128, 128), BF16),
            dma((6,)), dma((6,)),
            dma((N_STEPS,)), dma((N_STEPS,)), dma((N_STEPS,)), dma((N_STEPS,)),
            dma((SUBS - 1,)), dma((SUBS - 1,)),
            dma((XS - 1,)), dma((XS - 1,)),
            dma((XS,)), dma((XS,)),
            dma((7,)), dma((1,)),
        ],
        compiler_params=pltpu.CompilerParams(
            collective_id=0, has_side_effects=True, vmem_limit_bytes=VMEM_LIMIT
        ),
        name="comm_fields",
    )(masked, c0, c1, c2, c35, c6, coupling, near_tiles, far, near)


BLOCK = 8


def down_kernel(cnt, fields, e, nearby, bas, out, d):
    g = pl.program_id(0)

    def lower(level, low, count):
        start, _ = span(level)
        parents, _ = span(level + 1)

        def parent(i, carry):
            p = low + i
            pair = e[pl.ds(start + 2 * p, 2)].reshape(128, 64)
            got = jnp.dot(pair, d[parents + p], preferred_element_type=F32)
            got = got + fields[pl.ds(start + 2 * p, 2)].reshape(128, 128)
            d[pl.ds(start + 2 * p, 2)] = got.reshape(2, 64, 128).astype(BF16)
            return carry

        lax.fori_loop(0, count, parent, 0, unroll=min(count, 4))

    @pl.when(g == 0)
    def _():
        d[126] = fields[126].astype(BF16)
        for level in range(LEVELS - 1, 0, -1):
            lower(level, 0, span(level + 1)[1])

    lower(0, g * (BLOCK // 2), BLOCK // 2)
    lane = lax.broadcasted_iota(jnp.int32, (1, 128), 1)
    for i in range(BLOCK):
        l = g * BLOCK + i
        smooth = lax.dot_general(d[l], bas[i], TN, preferred_element_type=F32)
        live = (lane < cnt[0, l]).astype(F32)
        out[:, i * 128 : (i + 1) * 128] = (smooth + nearby[i].astype(F32)) * live


def down_pass(cnt, fields, e, nearby, bas):
    return pl.pallas_call(
        down_kernel,
        grid=(64 // BLOCK,),
        out_shape=jax.ShapeDtypeStruct((128, 8192), F32),
        in_specs=[
            pl.BlockSpec(memory_space=pltpu.SMEM),
            pl.BlockSpec(memory_space=pltpu.VMEM),
            pl.BlockSpec(memory_space=pltpu.VMEM),
            pl.BlockSpec((BLOCK, 128, 128), lambda g: (g, 0, 0)),
            pl.BlockSpec((BLOCK, 64, 128), lambda g: (g, 0, 0)),
        ],
        out_specs=pl.BlockSpec((128, BLOCK * 128), lambda g: (0, g)),
        scratch_shapes=[pltpu.VMEM((127, 64, 128), BF16)],
        compiler_params=pltpu.CompilerParams(vmem_limit_bytes=VMEM_LIMIT),
        name="down_pass",
    )(cnt, fields, e, nearby, bas)


def body(
    currents,
    leaf_segment_count,
    leaf_basis,
    transfers,
    coupling,
    far_sources,
    near_tiles,
    near_sources,
):
    basis = jnp.transpose(leaf_basis, (0, 2, 1))
    tr = jnp.transpose(transfers, (1, 2, 0))
    matrices = jnp.transpose(coupling, (1, 2, 3, 0))
    far = jnp.transpose(far_sources, (1, 0))
    near = jnp.transpose(near_sources, (1, 0))
    masked, c0, c1, c2, c35, c6, e = up_pass(leaf_segment_count, currents, basis, tr)
    fields, nearby = comm_fields(masked, c0, c1, c2, c35, c6, matrices, near_tiles, far, near)
    return down_pass(leaf_segment_count, fields, e, nearby, basis)


def solution(mesh):
    return jax.shard_map(
        body,
        mesh=mesh,
        in_specs=(
            P(None, ("grp", "sub")),
            P(("grp", "sub"), None),
            P(("grp", "sub"), None, None),
            P(("grp", "sub"), None, None),
            P(("grp", "sub"), None, None, None),
            P(("grp", "sub"), None),
            P(("grp", "sub"), None, None, None),
            P(("grp", "sub"), None),
        ),
        out_specs=P(None, ("grp", "sub")),
        check_vma=False,
    )
```

```python
import functools

import jax
import jax.numpy as jnp
from jax import lax
from jax.experimental import pallas as pl
from jax.experimental.pallas import tpu as pltpu
from jax.sharding import PartitionSpec as P

LEVELS = 6
REACH = 8
NEAR_REACH = 2
SIDE = 4
SUBS = 16
XS = 4
F32 = jnp.float32
BF16 = jnp.bfloat16
VMEM_LIMIT = 60 * 1024 * 1024

C_STRIDE = 72
C_ROWS = 127 * C_STRIDE
E_STRIDE = 40
NT = (((1,), (1,)), ((), ()))
TN = (((0,), (0,)), ((), ()))


def span(level):
    count = 64 >> level
    return 128 - 2 * count, count


STEPS = (
    (None, 0, 0, 0, 0, 1),
    (None, 0, 0, 0, 0, -1),
    (None, 0, 0, 0, 1, 1),
    (None, 0, 0, 0, 1, -1),
    (0, -1, 0, 1, 0, 1),
    (0, -1, 0, 0, 1, 1),
    (0, -1, 0, 0, 1, -1),
    (1, 1, 0, 2, 0, -1),
    (1, 1, 0, 0, 1, 1),
    (1, 1, 0, 0, 1, -1),
    (2, 0, -1, 1, 1, 1),
    (3, 0, 1, 2, 1, -1),
    (4, 2, 0, 1, 1, 1),
    (4, 2, 0, 1, 1, -1),
    (7, 2, 0, 2, 1, 1),
    (7, 2, 0, 2, 1, -1),
    (8, 1, -1, 0, 1, 1),
    (6, -1, 1, 0, 1, -1),
    (12, 2, -1, 1, 1, 1),
    (15, 2, 1, 2, 1, -1),
)
N_STEPS = len(STEPS)
WAVES = ((0, 1, 2, 3), (4, 7, 8, 6), (12, 15), (5, 9, 10, 11, 13, 14, 16, 17, 18, 19))

TREES = (
    ("g2", 16, 0, 8, True),
    ("g2", 16, 8, 8, False),
    ("g35", 14, 0, 8, True),
    ("g35", 14, 8, 6, False),
)
CHUNKS = 8


def main_kernel(
    cnt, currents, basis, transfers, coupling, near_tiles, far, near,
    partial_out, joined_out, d1_out,
    cur, bas, tr, e32, xm, x0, x1, g2, g35, roots, cin, c32, tiles, fields, partial, joined, d,
    in_sem, out_sem, halo_send, halo_recv, tree_send, tree_recv,
    root_send, root_recv, xs_send, xs_recv, core_send, core_recv,
):
    grp = lax.axis_index("grp")
    sub = lax.axis_index("sub")
    y = sub // SIDE
    z = sub % SIDE
    core = grp % 2
    x = grp // 2
    mine = grp * SUBS + sub

    def at(dy, dz):
        return ((y + dy + SIDE) % SIDE) * SIDE + (z + dz + SIDE) % SIDE

    def along_x(i):
        return ((x + i) % XS) * 2 + core

    other_core = x * 2 + (1 - core)

    loads = [
        pltpu.make_async_copy(src, dst, in_sem.at[i])
        for i, (src, dst) in enumerate(
            ((transfers, tr), (currents, cur), (basis, bas), (coupling, cin), (near_tiles, tiles))
        )
    ]
    for copy in loads:
        copy.start()

    barrier = pltpu.get_barrier_semaphore()

    def greet(device):
        pl.semaphore_signal(
            barrier, inc=1, device_id=device, device_id_type=pl.DeviceIdType.MESH
        )

    for i in range(1, SUBS):
        greet((grp, (sub + i) % SUBS))
    for i in range(1, XS):
        greet((along_x(i), sub))
    greet((other_core, sub))

    def remote(src, dst, send, recv, device):
        return pltpu.make_async_remote_copy(
            src_ref=src, dst_ref=dst, send_sem=send, recv_sem=recv,
            device_id=device, device_id_type=pl.DeviceIdType.MESH,
        )

    up, down = (grp, (sub + 1) % SUBS), (grp, (sub + SUBS - 1) % SUBS)
    halos = []
    for i, (buffer, width, count) in enumerate(
        ((xm, NEAR_REACH, 64), (x0, REACH, 64), (x1, REACH, 32))
    ):
        halos.append(
            (
                remote(buffer.at[pl.ds(count, width)], buffer.at[pl.ds(0, width)],
                       halo_send.at[2 * i], halo_recv.at[2 * i], up),
                remote(buffer.at[pl.ds(width, width)], buffer.at[pl.ds(count + width, width)],
                       halo_send.at[2 * i + 1], halo_recv.at[2 * i + 1], down),
            )
        )

    def step_copy(tree, i):
        name, n, low, width, z_first = TREES[tree]
        buffer = g2 if name == "g2" else g35
        _, first, second, part, dim, way = STEPS[i]
        offset = (second, first) if z_first else (first, second)
        move = (way, 0) if (dim == 1) == z_first else (0, way)
        half = width // 2
        skip, rows = ((0, width), (0, half), (half, width - half))[part]
        block = buffer.at[pl.ds(at(*offset) * n + low + skip, rows)]
        return remote(block, block, tree_send.at[tree * N_STEPS + i],
                      tree_recv.at[tree * N_STEPS + i], (grp, at(*move)))

    copies = [[step_copy(tree, i) for i in range(N_STEPS)] for tree in range(len(TREES))]

    def begin(tree):
        for i in range(4):
            copies[tree][i].start()

    def wave(tree, k):
        for i in WAVES[k]:
            copies[tree][i].wait_recv()
            for j in range(N_STEPS):
                if STEPS[j][0] == i:
                    copies[tree][j].start()


    def relayout_e(k, carry):
        slab = jnp.concatenate([tr[k], tr[k + 32]], axis=0).astype(F32)
        e32[pl.ds(k, 126, stride=E_STRIDE), :] = slab.T
        return carry

    def transfer(t, count):
        parts = []
        for c in range(count):
            rows = e32[pl.ds(pl.multiple_of((t + c) * E_STRIDE, 8), 32), :].astype(BF16)
            parts += [rows[:, :64], rows[:, 64:]]
        return jnp.concatenate(parts, axis=0)

    loads[0].wait()
    lax.fori_loop(0, 32, relayout_e, 0, unroll=4)
    loads[1].wait()
    loads[2].wait()

    lane = lax.broadcasted_iota(jnp.int32, (1, 128), 1)

    def leaf(l, carry):
        live = (lane < cnt[0, l]).astype(F32).astype(BF16)
        m = cur[:, pl.ds(pl.multiple_of(l * 128, 128), 128)] * live
        xm[NEAR_REACH + l] = m
        c = lax.dot_general(bas[l], m, NT, preferred_element_type=F32)
        x0[REACH + l] = c.astype(BF16)
        return carry

    def lift(level, src, src_at, dst, dst_at, low, count, unroll):
        start, _ = span(level - 1)

        def parent(i, carry):
            p = low + i
            pair = src[pl.ds(src_at + 2 * p, 2)].reshape(128, 128)
            c = lax.dot_general(transfer(start + 2 * p, 2), pair, TN, preferred_element_type=F32)
            dst[dst_at + p] = c.astype(BF16)
            return carry

        lax.fori_loop(0, count, parent, 0, unroll=unroll)

    slot2, slot35 = sub * 16, sub * 14
    for h in range(2):
        lax.fori_loop(32 * h, 32 * (h + 1), leaf, 0, unroll=8)
        if h == 0:
            pl.semaphore_wait(barrier, SUBS - 1 + XS - 1 + 1)
        halos[0][1 - h].start()
        halos[1][1 - h].start()
        lift(1, x0, REACH, x1, REACH, 16 * h, 16, 8)
        halos[2][1 - h].start()
        lift(2, x1, REACH, g2, slot2, 8 * h, 8, 8)
        begin(h)
    lift(3, g2, slot2, g35, slot35, 0, 8, 8)
    begin(2)
    lift(4, g35, slot35, g35, slot35 + 8, 0, 4, 4)
    lift(5, g35, slot35 + 8, g35, slot35 + 12, 0, 2, 2)
    begin(3)
    lift(6, g35, slot35 + 12, roots, mine, 0, 1, 1)
    root_row = roots.at[pl.ds(mine, 1)]
    root_copies = [
        remote(root_row, root_row, root_send.at[i - 1], root_recv.at[i - 1],
               (grp, (sub + i) % SUBS))
        for i in range(1, SUBS)
    ]
    for copy in root_copies:
        copy.start()


    def relayout_c(low, high):
        def one(a, carry):
            for qp in range(3):
                slab = cin[pl.ds(2 * qp, 2), a].reshape(128, 127).astype(F32)
                c32[pl.ds(qp * C_ROWS + a, 127, stride=C_STRIDE), :] = slab.T
            return carry

        lax.fori_loop(low, high, one, 0, unroll=2)

    def couple(level, buffer, place, low, count, unroll):
        start, _ = span(level)
        last = buffer.shape[0] - 1

        def target(i, carry):
            t = start + low + i
            matrix = jnp.concatenate(
                [
                    c32[pl.ds(pl.multiple_of(qp * C_ROWS + t * C_STRIDE, 8), 64), :].astype(BF16)
                    for qp in range(3)
                ],
                axis=1,
            )
            stacked = jnp.concatenate(
                [buffer[jnp.clip(place(far[q, t]), 0, last)] for q in range(6)], axis=0
            )
            fields[t] = jnp.dot(matrix, stacked, preferred_element_type=F32)
            return carry

        lax.fori_loop(0, count, target, 0, unroll=unroll)

    def join(low, count):
        def one(i, carry):
            l = low + i
            got = lax.dot_general(transfer(l, 1), bas[l], TN, preferred_element_type=F32)
            joined[l] = got.astype(BF16)
            return carry

        lax.fori_loop(0, count, one, 0, unroll=4)

    near_base = mine * 64 - NEAR_REACH
    outs = []

    def near_field(low, count):
        def one(i, carry):
            t = low + i
            total = lax.dot_general(
                fields[t].astype(BF16), bas[t], TN, preferred_element_type=F32
            )
            rows = jnp.concatenate(
                [
                    xm[jnp.clip(near[q, t] - near_base, 0, 64 + 2 * NEAR_REACH - 1)]
                    for q in range(5)
                ],
                axis=1,
            )
            blocks = jnp.concatenate([tiles[t, q] for q in range(5)], axis=1)
            total = total + lax.dot_general(rows, blocks, NT, preferred_element_type=F32)
            partial[t] = total.astype(BF16)
            return carry

        lax.fori_loop(0, count, one, 0, unroll=4)
        block = pl.ds(low, count)
        copy = pltpu.make_async_copy(
            partial.at[block], partial_out.at[block], out_sem.at[1 + low // count]
        )
        copy.start()
        outs.append(copy)

    place0 = lambda s: s - (mine * 64 - REACH)
    place1 = lambda s: s - (mine * 32 - REACH)

    loads[3].wait()
    relayout_c(0, 16)
    wave(0, 0)
    relayout_c(16, 32)
    wave(1, 0)
    relayout_c(32, 48)
    wave(2, 0)
    relayout_c(48, 64)
    wave(3, 0)

    for copy in root_copies:
        copy.wait_recv()
    block = roots.at[pl.ds(grp * SUBS, SUBS)]
    x_copies = [
        remote(block, block, xs_send.at[i - 1], xs_recv.at[i - 1], (along_x(i), sub))
        for i in range(1, XS)
    ]
    for copy in x_copies:
        copy.start()
    core_copies = []
    for i in range(XS):
        held = roots.at[pl.ds(along_x(i) * SUBS, SUBS)]
        core_copies.append(
            remote(held, held, core_send.at[i], core_recv.at[i], (other_core, sub))
        )
    core_copies[0].start()

    for i in range(2):
        halos[1][i].wait_recv()
    couple(0, x0, place0, 0, 32, 8)
    wave(0, 1)
    couple(0, x0, place0, 32, 32, 8)
    wave(1, 1)
    join(0, 64)
    copy = pltpu.make_async_copy(joined, joined_out, out_sem.at[0])
    copy.start()
    outs.append(copy)
    wave(2, 1)
    loads[4].wait()
    for i in range(2):
        halos[0][i].wait_recv()
    width = 64 // CHUNKS
    near_field(0, width)
    near_field(width, width)
    wave(3, 1)
    near_field(2 * width, width)
    near_field(3 * width, width)
    wave(0, 2)
    near_field(4 * width, width)
    near_field(5 * width, width)
    wave(1, 2)
    near_field(6 * width, width)
    near_field(7 * width, width)
    wave(2, 2)
    for copy in x_copies:
        copy.wait_recv()
    for copy in core_copies[1:]:
        copy.start()
    for i in range(2):
        halos[2][i].wait_recv()
    couple(1, x1, place1, 0, 32, 8)
    wave(3, 2)
    for copy in core_copies:
        copy.wait_recv()
    couple(6, roots, lambda s: s, 0, 1, 1)

    def place35(level, offset):
        _, count = span(level)

        def place(s):
            relative = s - grp * SUBS * count
            return (relative // count) * 14 + offset + relative % count

        return place

    wave(2, 3)
    wave(3, 3)
    couple(3, g35, place35(3, 0), 0, 8, 8)
    couple(4, g35, place35(4, 8), 0, 4, 4)
    couple(5, g35, place35(5, 12), 0, 2, 2)
    wave(0, 3)
    wave(1, 3)
    couple(2, g2, lambda s: s - grp * SUBS * 16, 0, 16, 8)


    d[126] = fields[126].astype(BF16)
    for level in range(LEVELS - 1, 0, -1):
        start, _ = span(level)
        parents, count = span(level + 1)

        def parent(p, carry, start=start, parents=parents, level=level):
            got = jnp.dot(
                transfer(start + 2 * p, 2), d[parents + p], preferred_element_type=F32
            )
            got = got + fields[pl.ds(start + 2 * p, 2)].reshape(128, 128)
            got = got.reshape(2, 64, 128).astype(BF16)
            if level == 1:
                d1_out[pl.ds(2 * p, 2)] = got
            else:
                d[pl.ds(start + 2 * p, 2)] = got
            return carry

        lax.fori_loop(0, count, parent, 0, unroll=min(count, 8))

    for copy in root_copies + [c for pair in halos for c in pair] + x_copies + core_copies:
        copy.wait_send()
    for tree in copies:
        for copy in tree:
            copy.wait_send()
    for copy in outs:
        copy.wait()


def main_pass(cnt, currents, basis, tr, matrices, near_tiles, far, near):
    vm = pl.BlockSpec(memory_space=pltpu.VMEM)
    hbm = pl.BlockSpec(memory_space=pl.ANY)
    sm = pl.BlockSpec(memory_space=pltpu.SMEM)
    dma = pltpu.SemaphoreType.DMA
    steps = len(TREES) * N_STEPS
    return pl.pallas_call(
        main_kernel,
        out_shape=(
            jax.ShapeDtypeStruct((64, 128, 128), BF16),
            jax.ShapeDtypeStruct((64, 64, 128), BF16),
            jax.ShapeDtypeStruct((32, 64, 128), BF16),
        ),
        in_specs=[sm, hbm, hbm, hbm, hbm, hbm, sm, sm],
        out_specs=(hbm, hbm, vm),
        scratch_shapes=[
            pltpu.VMEM((128, 8192), BF16),
            pltpu.VMEM((64, 64, 128), BF16),
            pltpu.VMEM((64, 64, 126), BF16),
            pltpu.VMEM((126 * E_STRIDE, 128), F32),
            pltpu.VMEM((64 + 2 * NEAR_REACH, 128, 128), BF16),
            pltpu.VMEM((64 + 2 * REACH, 64, 128), BF16),
            pltpu.VMEM((32 + 2 * REACH, 64, 128), BF16),
            pltpu.VMEM((256, 64, 128), BF16),
            pltpu.VMEM((224, 64, 128), BF16),
            pltpu.VMEM((128, 64, 128), BF16),
            pltpu.VMEM((6, 64, 64, 127), BF16),
            pltpu.VMEM((3 * C_ROWS, 128), F32),
            pltpu.VMEM((64, 5, 128, 128), BF16),
            pltpu.VMEM((127, 64, 128), F32),
            pltpu.VMEM((64, 128, 128), BF16),
            pltpu.VMEM((64, 64, 128), BF16),
            pltpu.VMEM((127, 64, 128), BF16),
            dma((5,)), dma((1 + CHUNKS,)),
            dma((6,)), dma((6,)),
            dma((steps,)), dma((steps,)),
            dma((SUBS - 1,)), dma((SUBS - 1,)),
            dma((XS - 1,)), dma((XS - 1,)),
            dma((XS,)), dma((XS,)),
        ],
        compiler_params=pltpu.CompilerParams(
            collective_id=0, has_side_effects=True, vmem_limit_bytes=VMEM_LIMIT
        ),
        name="main_pass",
    )(cnt, currents, basis, tr, matrices, near_tiles, far, near)


BLOCK = 8


def last_kernel(cnt, d1, joined, partial, out):
    g = pl.program_id(0)
    lane = lax.broadcasted_iota(jnp.int32, (1, 128), 1)
    for i in range(BLOCK):
        smooth = lax.dot_general(d1[i // 2], joined[i], TN, preferred_element_type=F32)
        live = (lane < cnt[0, g * BLOCK + i]).astype(F32)
        out[:, i * 128 : (i + 1) * 128] = (smooth + partial[i].astype(F32)) * live


def last_pass(cnt, d1, joined, partial):
    return pl.pallas_call(
        last_kernel,
        grid=(64 // BLOCK,),
        out_shape=jax.ShapeDtypeStruct((128, 8192), F32),
        in_specs=[
            pl.BlockSpec(memory_space=pltpu.SMEM),
            pl.BlockSpec((BLOCK // 2, 64, 128), lambda g: (g, 0, 0)),
            pl.BlockSpec((BLOCK, 64, 128), lambda g: (g, 0, 0)),
            pl.BlockSpec((BLOCK, 128, 128), lambda g: (g, 0, 0)),
        ],
        out_specs=pl.BlockSpec((128, BLOCK * 128), lambda g: (0, g)),
        compiler_params=pltpu.CompilerParams(vmem_limit_bytes=VMEM_LIMIT),
        name="last_pass",
    )(cnt, d1, joined, partial)


def body(
    currents,
    leaf_segment_count,
    leaf_basis,
    transfers,
    coupling,
    far_sources,
    near_tiles,
    near_sources,
):
    basis = jnp.transpose(leaf_basis, (0, 2, 1))
    tr = jnp.transpose(transfers, (1, 2, 0))
    matrices = jnp.transpose(coupling, (1, 2, 3, 0))
    far = jnp.transpose(far_sources, (1, 0))
    near = jnp.transpose(near_sources, (1, 0))
    partial, joined, d1 = main_pass(
        leaf_segment_count, currents, basis, tr, matrices, near_tiles, far, near
    )
    return last_pass(leaf_segment_count, d1, joined, partial)


def solution(mesh):
    return jax.shard_map(
        body,
        mesh=mesh,
        in_specs=(
            P(None, ("grp", "sub")),
            P(("grp", "sub"), None),
            P(("grp", "sub"), None, None),
            P(("grp", "sub"), None, None),
            P(("grp", "sub"), None, None, None),
            P(("grp", "sub"), None),
            P(("grp", "sub"), None, None, None),
            P(("grp", "sub"), None),
        ),
        out_specs=P(None, ("grp", "sub")),
        check_vma=False,
    )
```

```python
import functools

import jax
import jax.numpy as jnp
from jax import lax
from jax.experimental import pallas as pl
from jax.experimental.pallas import tpu as pltpu
from jax.sharding import PartitionSpec as P

LEVELS = 6
REACH = 8
NEAR_REACH = 2
SIDE = 4
SUBS = 16
XS = 4
F32 = jnp.float32
BF16 = jnp.bfloat16
VMEM_LIMIT = 60 * 1024 * 1024

C_STRIDE = 72
C_ROWS = 127 * C_STRIDE
E_STRIDE = 40
ROOT_ROWS = 4
NT = (((1,), (1,)), ((), ()))
TN = (((0,), (0,)), ((), ()))


def span(level):
    count = 64 >> level
    return 128 - 2 * count, count


STEPS = (
    (None, 0, 0, 0, 0, 1),
    (None, 0, 0, 0, 0, -1),
    (None, 0, 0, 0, 1, 1),
    (None, 0, 0, 0, 1, -1),
    (0, -1, 0, 1, 0, 1),
    (0, -1, 0, 0, 1, 1),
    (0, -1, 0, 0, 1, -1),
    (1, 1, 0, 2, 0, -1),
    (1, 1, 0, 0, 1, 1),
    (1, 1, 0, 0, 1, -1),
    (2, 0, -1, 1, 1, 1),
    (3, 0, 1, 2, 1, -1),
    (4, 2, 0, 1, 1, 1),
    (4, 2, 0, 1, 1, -1),
    (7, 2, 0, 2, 1, 1),
    (7, 2, 0, 2, 1, -1),
    (8, 1, -1, 0, 1, 1),
    (6, -1, 1, 0, 1, -1),
    (12, 2, -1, 1, 1, 1),
    (15, 2, 1, 2, 1, -1),
)
N_STEPS = len(STEPS)
WAVES = ((0, 1, 2, 3), (4, 7, 8, 6), (12, 15), (5, 9, 10, 11, 13, 14, 16, 17, 18, 19))

TREES = (
    ("g2", 16, 0, 8, True),
    ("g2", 16, 8, 8, False),
    ("g35", 14, 0, 8, True),
    ("g35", 14, 8, 6, False),
    ("roots", ROOT_ROWS, 0, ROOT_ROWS, True),
)
ROOT_TREE = 4
CHUNKS = 8


def main_kernel(
    cnt, currents, basis, transfers, coupling, near_tiles, far, near,
    partial_out, joined_out, d2_out,
    cur, bas, tr, e32, xm, x0, x1, g2, g35, roots, cin, c32, tiles, fields, partial, joined, joined2, d,
    in_sem, out_sem, halo_send, halo_recv, tree_send, tree_recv,
    xs_send, xs_recv, core_send, core_recv,
):
    grp = lax.axis_index("grp")
    sub = lax.axis_index("sub")
    y = sub // SIDE
    z = sub % SIDE
    core = grp % 2
    x = grp // 2
    mine = grp * SUBS + sub

    def at(dy, dz):
        return ((y + dy + SIDE) % SIDE) * SIDE + (z + dz + SIDE) % SIDE

    def along_x(i):
        return ((x + i) % XS) * 2 + core

    other_core = x * 2 + (1 - core)

    loads = [
        pltpu.make_async_copy(src, dst, in_sem.at[i])
        for i, (src, dst) in enumerate(
            ((transfers, tr), (currents, cur), (basis, bas), (coupling, cin), (near_tiles, tiles))
        )
    ]
    for copy in loads:
        copy.start()

    barrier = pltpu.get_barrier_semaphore()

    def greet(device):
        pl.semaphore_signal(
            barrier, inc=1, device_id=device, device_id_type=pl.DeviceIdType.MESH
        )

    for i in range(1, SUBS):
        greet((grp, (sub + i) % SUBS))
    for i in range(1, XS):
        greet((along_x(i), sub))
    greet((other_core, sub))

    def remote(src, dst, send, recv, device):
        return pltpu.make_async_remote_copy(
            src_ref=src, dst_ref=dst, send_sem=send, recv_sem=recv,
            device_id=device, device_id_type=pl.DeviceIdType.MESH,
        )

    up, down = (grp, (sub + 1) % SUBS), (grp, (sub + SUBS - 1) % SUBS)
    halos = []
    for i, (buffer, width, count) in enumerate(
        ((xm, NEAR_REACH, 64), (x0, REACH, 64), (x1, REACH, 32))
    ):
        halos.append(
            (
                remote(buffer.at[pl.ds(count, width)], buffer.at[pl.ds(0, width)],
                       halo_send.at[2 * i], halo_recv.at[2 * i], up),
                remote(buffer.at[pl.ds(width, width)], buffer.at[pl.ds(count + width, width)],
                       halo_send.at[2 * i + 1], halo_recv.at[2 * i + 1], down),
            )
        )

    def step_copy(tree, i):
        name, n, low, width, z_first = TREES[tree]
        buffer = {"g2": g2, "g35": g35, "roots": roots}[name]
        _, first, second, part, dim, way = STEPS[i]
        offset = (second, first) if z_first else (first, second)
        move = (way, 0) if (dim == 1) == z_first else (0, way)
        half = width // 2
        skip, rows = ((0, width), (0, half), (half, width - half))[part]
        slot = at(*offset) + (grp * SUBS if name == "roots" else 0)
        block = buffer.at[pl.ds(slot * n + low + skip, rows)]
        return remote(block, block, tree_send.at[tree * N_STEPS + i],
                      tree_recv.at[tree * N_STEPS + i], (grp, at(*move)))

    copies = [[step_copy(tree, i) for i in range(N_STEPS)] for tree in range(len(TREES))]

    def begin(tree):
        for i in range(4):
            copies[tree][i].start()

    def wave(tree, k):
        for i in WAVES[k]:
            copies[tree][i].wait_recv()
            for j in range(N_STEPS):
                if STEPS[j][0] == i:
                    copies[tree][j].start()


    def relayout_e(k, carry):
        slab = jnp.concatenate([tr[k], tr[k + 32]], axis=0).astype(F32)
        e32[pl.ds(k, 126, stride=E_STRIDE), :] = slab.T
        return carry

    def transfer(t, count):
        parts = []
        for c in range(count):
            rows = e32[pl.ds(pl.multiple_of((t + c) * E_STRIDE, 8), 32), :].astype(BF16)
            parts += [rows[:, :64], rows[:, 64:]]
        return jnp.concatenate(parts, axis=0)

    loads[0].wait()
    lax.fori_loop(0, 32, relayout_e, 0, unroll=4)
    loads[1].wait()
    loads[2].wait()

    lane = lax.broadcasted_iota(jnp.int32, (1, 128), 1)

    def leaf(l, carry):
        live = (lane < cnt[0, l]).astype(F32).astype(BF16)
        m = cur[:, pl.ds(pl.multiple_of(l * 128, 128), 128)] * live
        xm[NEAR_REACH + l] = m
        c = lax.dot_general(bas[l], m, NT, preferred_element_type=F32)
        x0[REACH + l] = c.astype(BF16)
        return carry

    def lift(level, src, src_at, dst, dst_at, low, count, unroll):
        start, _ = span(level - 1)

        def parent(i, carry):
            p = low + i
            pair = src[pl.ds(src_at + 2 * p, 2)].reshape(128, 128)
            c = lax.dot_general(transfer(start + 2 * p, 2), pair, TN, preferred_element_type=F32)
            dst[dst_at + p] = c.astype(BF16)
            return carry

        lax.fori_loop(0, count, parent, 0, unroll=unroll)

    slot2, slot35 = sub * 16, sub * 14
    for h in range(2):
        lax.fori_loop(32 * h, 32 * (h + 1), leaf, 0, unroll=8)
        if h == 0:
            pl.semaphore_wait(barrier, SUBS - 1 + XS - 1 + 1)
        halos[0][1 - h].start()
        halos[1][1 - h].start()
        lift(1, x0, REACH, x1, REACH, 16 * h, 16, 8)
        halos[2][1 - h].start()
        lift(2, x1, REACH, g2, slot2, 8 * h, 8, 8)
        if h == 0:
            begin(0)
    lift(3, g2, slot2, g35, slot35, 0, 8, 8)
    lift(4, g35, slot35, g35, slot35 + 8, 0, 4, 4)
    lift(5, g35, slot35 + 8, g35, slot35 + 12, 0, 2, 2)
    start6, _ = span(LEVELS - 1)
    pair = g35[pl.ds(slot35 + 12, 2)].reshape(128, 128)
    root = lax.dot_general(transfer(start6, 2), pair, TN, preferred_element_type=F32)
    roots[pl.ds(mine * ROOT_ROWS, ROOT_ROWS)] = root.astype(BF16).reshape(ROOT_ROWS, 16, 128)
    begin(ROOT_TREE)
    begin(3)
    begin(2)
    begin(1)


    def relayout_c(low, high):
        def one(a, carry):
            for qp in range(3):
                slab = cin[pl.ds(2 * qp, 2), a].reshape(128, 127).astype(F32)
                c32[pl.ds(qp * C_ROWS + a, 127, stride=C_STRIDE), :] = slab.T
            return carry

        lax.fori_loop(low, high, one, 0, unroll=2)

    def couple(level, buffer, place, low, count, unroll):
        start, _ = span(level)
        rows = ROOT_ROWS if level == LEVELS else 1
        last = buffer.shape[0] // rows - 1

        def source(q, t):
            i = jnp.clip(place(far[q, t]), 0, last)
            return buffer[i] if rows == 1 else buffer[pl.ds(i * rows, rows)].reshape(64, 128)

        def target(i, carry):
            t = start + low + i
            matrix = jnp.concatenate(
                [
                    c32[pl.ds(pl.multiple_of(qp * C_ROWS + t * C_STRIDE, 8), 64), :].astype(BF16)
                    for qp in range(3)
                ],
                axis=1,
            )
            stacked = jnp.concatenate([source(q, t) for q in range(6)], axis=0)
            got = jnp.dot(matrix, stacked, preferred_element_type=F32)
            if level == 2:
                d2_out[low + i] = (fields[t] + got).astype(BF16)
            else:
                fields[t] = got
            return carry

        lax.fori_loop(0, count, target, 0, unroll=unroll)

    def join(low, count):
        def one(i, carry):
            p = low + i
            pair = []
            for c in range(2):
                l = 2 * p + c
                got = lax.dot_general(transfer(l, 1), bas[l], TN, preferred_element_type=F32)
                pair.append(got.astype(BF16))
                joined[l] = pair[-1]
            got = lax.dot_general(
                transfer(64 + p, 1), jnp.concatenate(pair, axis=1), TN,
                preferred_element_type=F32,
            ).astype(BF16)
            joined2[2 * p] = got[:, :128]
            joined2[2 * p + 1] = got[:, 128:]
            return carry

        lax.fori_loop(0, count, one, 0, unroll=4)

    near_base = mine * 64 - NEAR_REACH
    outs = []

    def near_field(low, count):
        def one(i, carry):
            t = low + i
            both = jnp.concatenate([fields[t], fields[64 + t // 2]], axis=0).astype(BF16)
            total = lax.dot_general(
                both, jnp.concatenate([bas[t], joined[t]], axis=0), TN,
                preferred_element_type=F32,
            )
            rows = jnp.concatenate(
                [
                    xm[jnp.clip(near[q, t] - near_base, 0, 64 + 2 * NEAR_REACH - 1)]
                    for q in range(5)
                ],
                axis=1,
            )
            blocks = jnp.concatenate([tiles[t, q] for q in range(5)], axis=1)
            total = total + lax.dot_general(rows, blocks, NT, preferred_element_type=F32)
            partial[t] = total.astype(BF16)
            return carry

        lax.fori_loop(0, count, one, 0, unroll=4)
        block = pl.ds(low, count)
        copy = pltpu.make_async_copy(
            partial.at[block], partial_out.at[block], out_sem.at[1 + low // count]
        )
        copy.start()
        outs.append(copy)

    place0 = lambda s: s - (mine * 64 - REACH)
    place1 = lambda s: s - (mine * 32 - REACH)

    loads[3].wait()
    relayout_c(0, 16)
    wave(0, 0)
    wave(ROOT_TREE, 0)
    relayout_c(16, 32)
    wave(3, 0)
    wave(ROOT_TREE, 1)
    relayout_c(32, 48)
    wave(2, 0)
    wave(ROOT_TREE, 2)
    relayout_c(48, 64)
    wave(1, 0)
    wave(ROOT_TREE, 3)

    def group_roots(g):
        return roots.at[pl.ds(g * SUBS * ROOT_ROWS, SUBS * ROOT_ROWS)]

    block = group_roots(grp)
    x_copies = [
        remote(block, block, xs_send.at[i - 1], xs_recv.at[i - 1], (along_x(i), sub))
        for i in range(1, XS)
    ]
    for copy in x_copies:
        copy.start()
    core_copies = [
        remote(group_roots(along_x(i)), group_roots(along_x(i)), core_send.at[i],
               core_recv.at[i], (other_core, sub))
        for i in range(XS)
    ]
    core_copies[0].start()

    for i in range(2):
        halos[1][i].wait_recv()
    couple(0, x0, place0, 0, 32, 8)
    wave(0, 1)
    couple(0, x0, place0, 32, 32, 8)
    wave(3, 1)
    for i in range(2):
        halos[2][i].wait_recv()
    couple(1, x1, place1, 0, 32, 8)
    wave(2, 1)
    join(0, 16)
    wave(1, 1)
    join(16, 16)
    copy = pltpu.make_async_copy(joined2, joined_out, out_sem.at[0])
    copy.start()
    outs.append(copy)
    wave(0, 2)
    loads[4].wait()
    for i in range(2):
        halos[0][i].wait_recv()
    width = 64 // CHUNKS
    near_field(0, width)
    near_field(width, width)
    wave(3, 2)
    near_field(2 * width, width)
    near_field(3 * width, width)
    wave(2, 2)
    near_field(4 * width, width)
    near_field(5 * width, width)
    wave(1, 2)
    near_field(6 * width, width)
    near_field(7 * width, width)
    for copy in x_copies:
        copy.wait_recv()
    for copy in core_copies[1:]:
        copy.start()
    for copy in core_copies:
        copy.wait_recv()
    couple(6, roots, lambda s: s, 0, 1, 1)

    def place35(level, offset):
        _, count = span(level)

        def place(s):
            relative = s - grp * SUBS * count
            return (relative // count) * 14 + offset + relative % count

        return place

    wave(3, 3)
    wave(2, 3)
    couple(5, g35, place35(5, 12), 0, 2, 2)
    couple(4, g35, place35(4, 8), 0, 4, 4)
    couple(3, g35, place35(3, 0), 0, 8, 8)


    d[126] = fields[126].astype(BF16)
    for level in range(LEVELS - 1, 1, -1):
        start, _ = span(level)
        parents, count = span(level + 1)

        def parent(p, carry, start=start, parents=parents, level=level):
            got = jnp.dot(
                transfer(start + 2 * p, 2), d[parents + p], preferred_element_type=F32
            )
            children = pl.ds(start + 2 * p, 2)
            if level == 2:
                fields[children] = got.reshape(2, 64, 128)
            else:
                got = got + fields[children].reshape(128, 128)
                d[children] = got.reshape(2, 64, 128).astype(BF16)
            return carry

        lax.fori_loop(0, count, parent, 0, unroll=count)

    wave(0, 3)
    wave(1, 3)
    couple(2, g2, lambda s: s - grp * SUBS * 16, 0, 16, 16)

    for copy in [c for pair in halos for c in pair] + x_copies + core_copies:
        copy.wait_send()
    for tree in copies:
        for copy in tree:
            copy.wait_send()
    for copy in outs:
        copy.wait()


def main_pass(cnt, currents, basis, tr, matrices, near_tiles, far, near):
    vm = pl.BlockSpec(memory_space=pltpu.VMEM)
    hbm = pl.BlockSpec(memory_space=pl.ANY)
    sm = pl.BlockSpec(memory_space=pltpu.SMEM)
    dma = pltpu.SemaphoreType.DMA
    steps = len(TREES) * N_STEPS
    return pl.pallas_call(
        main_kernel,
        out_shape=(
            jax.ShapeDtypeStruct((64, 128, 128), BF16),
            jax.ShapeDtypeStruct((64, 64, 128), BF16),
            jax.ShapeDtypeStruct((16, 64, 128), BF16),
        ),
        in_specs=[sm, hbm, hbm, hbm, hbm, hbm, sm, sm],
        out_specs=(hbm, hbm, vm),
        scratch_shapes=[
            pltpu.VMEM((128, 8192), BF16),
            pltpu.VMEM((64, 64, 128), BF16),
            pltpu.VMEM((64, 64, 126), BF16),
            pltpu.VMEM((126 * E_STRIDE, 128), F32),
            pltpu.VMEM((64 + 2 * NEAR_REACH, 128, 128), BF16),
            pltpu.VMEM((64 + 2 * REACH, 64, 128), BF16),
            pltpu.VMEM((32 + 2 * REACH, 64, 128), BF16),
            pltpu.VMEM((256, 64, 128), BF16),
            pltpu.VMEM((224, 64, 128), BF16),
            pltpu.VMEM((128 * ROOT_ROWS, 16, 128), BF16),
            pltpu.VMEM((6, 64, 64, 127), BF16),
            pltpu.VMEM((3 * C_ROWS, 128), F32),
            pltpu.VMEM((64, 5, 128, 128), BF16),
            pltpu.VMEM((127, 64, 128), F32),
            pltpu.VMEM((64, 128, 128), BF16),
            pltpu.VMEM((64, 64, 128), BF16),
            pltpu.VMEM((64, 64, 128), BF16),
            pltpu.VMEM((127, 64, 128), BF16),
            dma((5,)), dma((1 + CHUNKS,)),
            dma((6,)), dma((6,)),
            dma((steps,)), dma((steps,)),
            dma((XS - 1,)), dma((XS - 1,)),
            dma((XS,)), dma((XS,)),
        ],
        compiler_params=pltpu.CompilerParams(
            collective_id=0, has_side_effects=True, vmem_limit_bytes=VMEM_LIMIT
        ),
        name="main_pass",
    )(cnt, currents, basis, tr, matrices, near_tiles, far, near)


BLOCK = 32


def last_kernel(cnt, d2, joined, partial, out):
    g = pl.program_id(0)
    lane = lax.broadcasted_iota(jnp.int32, (1, 128), 1)
    for i in range(BLOCK):
        smooth = lax.dot_general(d2[i // 4], joined[i], TN, preferred_element_type=F32)
        live = (lane < cnt[0, g * BLOCK + i]).astype(F32)
        out[:, i * 128 : (i + 1) * 128] = (smooth + partial[i].astype(F32)) * live


def last_pass(cnt, d2, joined, partial):
    return pl.pallas_call(
        last_kernel,
        grid=(64 // BLOCK,),
        out_shape=jax.ShapeDtypeStruct((128, 8192), F32),
        in_specs=[
            pl.BlockSpec(memory_space=pltpu.SMEM),
            pl.BlockSpec((BLOCK // 4, 64, 128), lambda g: (g, 0, 0)),
            pl.BlockSpec((BLOCK, 64, 128), lambda g: (g, 0, 0)),
            pl.BlockSpec((BLOCK, 128, 128), lambda g: (g, 0, 0)),
        ],
        out_specs=pl.BlockSpec((128, BLOCK * 128), lambda g: (0, g)),
        compiler_params=pltpu.CompilerParams(vmem_limit_bytes=VMEM_LIMIT),
        name="last_pass",
    )(cnt, d2, joined, partial)


def body(
    currents,
    leaf_segment_count,
    leaf_basis,
    transfers,
    coupling,
    far_sources,
    near_tiles,
    near_sources,
):
    basis = jnp.transpose(leaf_basis, (0, 2, 1))
    tr = jnp.transpose(transfers, (1, 2, 0))
    matrices = jnp.transpose(coupling, (1, 2, 3, 0))
    far = jnp.transpose(far_sources, (1, 0))
    near = jnp.transpose(near_sources, (1, 0))
    partial, joined, d2 = main_pass(
        leaf_segment_count, currents, basis, tr, matrices, near_tiles, far, near
    )
    return last_pass(leaf_segment_count, d2, joined, partial)


def solution(mesh):
    return jax.shard_map(
        body,
        mesh=mesh,
        in_specs=(
            P(None, ("grp", "sub")),
            P(("grp", "sub"), None),
            P(("grp", "sub"), None, None),
            P(("grp", "sub"), None, None),
            P(("grp", "sub"), None, None, None),
            P(("grp", "sub"), None),
            P(("grp", "sub"), None, None, None),
            P(("grp", "sub"), None),
        ),
        out_specs=P(None, ("grp", "sub")),
        check_vma=False,
    )
```

```python
import functools

import jax
import jax.numpy as jnp
from jax import lax
from jax.experimental import pallas as pl
from jax.experimental.pallas import tpu as pltpu
from jax.sharding import PartitionSpec as P

LEVELS = 6
REACH = 8
NEAR_REACH = 2
SIDE = 4
SUBS = 16
XS = 4
F32 = jnp.float32
BF16 = jnp.bfloat16
VMEM_LIMIT = 60 * 1024 * 1024

C_STRIDE = 72
C_ROWS = 127 * C_STRIDE
E_STRIDE = 40
NT = (((1,), (1,)), ((), ()))
TN = (((0,), (0,)), ((), ()))


def span(level):
    count = 64 >> level
    return 128 - 2 * count, count


STEPS = (
    (None, 0, 0, 0, 0, 1),
    (None, 0, 0, 0, 0, -1),
    (None, 0, 0, 0, 1, 1),
    (None, 0, 0, 0, 1, -1),
    (0, -1, 0, 1, 0, 1),
    (0, -1, 0, 0, 1, 1),
    (0, -1, 0, 0, 1, -1),
    (1, 1, 0, 2, 0, -1),
    (1, 1, 0, 0, 1, 1),
    (1, 1, 0, 0, 1, -1),
    (2, 0, -1, 1, 1, 1),
    (3, 0, 1, 2, 1, -1),
    (4, 2, 0, 1, 1, 1),
    (4, 2, 0, 1, 1, -1),
    (7, 2, 0, 2, 1, 1),
    (7, 2, 0, 2, 1, -1),
    (8, 1, -1, 0, 1, 1),
    (6, -1, 1, 0, 1, -1),
    (12, 2, -1, 1, 1, 1),
    (15, 2, 1, 2, 1, -1),
)
N_STEPS = len(STEPS)

TREES = (
    ("g2", 16, 0, 8, True),
    ("g2", 16, 8, 8, False),
    ("g35", 14, 0, 7, True),
    ("g35", 14, 7, 7, False),
)
CHUNKS = 8


SCHEDULE = (
    ("r", 0), ("w", 0, 0), ("w", 0, 1), ("w", 0, 2), ("w", 0, 3), ("r", 1), ("w", 1, 0),
    ("w", 1, 1), ("w", 1, 2), ("w", 1, 3), ("r", 2), ("w", 2, 0), ("w", 2, 1), ("w", 2, 2),
    ("w", 2, 3), ("r", 3), ("w", 3, 0), ("w", 3, 1), ("w", 3, 2), ("w", 3, 3), ("rz",),
    ("c0", 0), ("c0", 1), ("w", 0, 4), ("w", 0, 7), ("w", 0, 8), ("w", 0, 6), ("c0", 2),
    ("c0", 3), ("w", 1, 4), ("w", 1, 7), ("w", 1, 8), ("w", 1, 6), ("c1", 0), ("c1", 1),
    ("j", 0), ("j", 1), ("w", 2, 4), ("w", 2, 7), ("w", 2, 8), ("w", 2, 6), ("j", 2), ("j", 3),
    ("n", 0), ("w", 3, 4), ("w", 3, 7), ("w", 3, 8), ("w", 3, 6), ("ry",), ("n", 1), ("n", 2),
    ("n", 3), ("w", 0, 12), ("w", 0, 15), ("n", 4), ("n", 5), ("w", 1, 12), ("w", 1, 15),
    ("n", 6), ("n", 7), ("w", 2, 12), ("w", 2, 15), ("rx",), ("w", 3, 12), ("w", 3, 15), ("rf",),
    ("rc",), ("w", 2, 5), ("w", 2, 9), ("w", 2, 10), ("w", 2, 11), ("w", 2, 13), ("w", 2, 14),
    ("w", 2, 16), ("w", 2, 17), ("w", 2, 18), ("w", 2, 19), ("w", 3, 5), ("w", 3, 9),
    ("w", 3, 10), ("w", 3, 11), ("w", 3, 13), ("w", 3, 14), ("w", 3, 16), ("w", 3, 17),
    ("w", 3, 18), ("w", 3, 19), ("f",), ("w", 0, 5), ("w", 0, 9), ("w", 0, 10), ("w", 0, 11),
    ("w", 0, 13), ("w", 0, 14), ("w", 0, 16), ("w", 0, 17), ("w", 0, 18), ("w", 0, 19),
    ("w", 1, 5), ("w", 1, 9), ("w", 1, 10), ("w", 1, 11), ("w", 1, 13), ("w", 1, 14),
    ("w", 1, 16), ("w", 1, 17), ("w", 1, 18), ("w", 1, 19),
)
HALO_OF = {"n": 0, "c0": 1, "c1": 2}


def main_kernel(
    cnt, currents, basis, transfers, coupling, near_tiles, far, near,
    partial_out, joined_out, d2_out,
    cur, bas, tr, e32, xm, x0, x1, g2, g35, roots, cin, c32, tiles, fields, partial, joined, joined2, d,
    in_sem, out_sem, halo_send, halo_recv, tree_send, tree_recv,
    root_send, root_recv,
):
    grp = lax.axis_index("grp")
    sub = lax.axis_index("sub")
    y = sub // SIDE
    z = sub % SIDE
    core = grp % 2
    x = grp // 2
    mine = grp * SUBS + sub

    def at(dy, dz):
        return ((y + dy + SIDE) % SIDE) * SIDE + (z + dz + SIDE) % SIDE

    def along_x(i):
        return ((x + i) % XS) * 2 + core

    other_core = x * 2 + (1 - core)

    loads = [
        pltpu.make_async_copy(src, dst, in_sem.at[i])
        for i, (src, dst) in enumerate(
            ((transfers, tr), (currents, cur), (basis, bas), (coupling, cin), (near_tiles, tiles))
        )
    ]
    for copy in loads:
        copy.start()

    barrier = pltpu.get_barrier_semaphore()

    def greet(device):
        pl.semaphore_signal(
            barrier, inc=1, device_id=device, device_id_type=pl.DeviceIdType.MESH
        )

    for i in range(1, SUBS):
        greet((grp, (sub + i) % SUBS))
    for i in range(1, XS):
        greet((along_x(i), sub))
    greet((other_core, sub))

    def remote(src, dst, send, recv, device):
        return pltpu.make_async_remote_copy(
            src_ref=src, dst_ref=dst, send_sem=send, recv_sem=recv,
            device_id=device, device_id_type=pl.DeviceIdType.MESH,
        )

    up, down = (grp, (sub + 1) % SUBS), (grp, (sub + SUBS - 1) % SUBS)
    halos = []
    for i, (buffer, width, count) in enumerate(
        ((xm, NEAR_REACH, 64), (x0, REACH, 64), (x1, REACH, 32))
    ):
        halos.append(
            (
                remote(buffer.at[pl.ds(count, width)], buffer.at[pl.ds(0, width)],
                       halo_send.at[2 * i], halo_recv.at[2 * i], up),
                remote(buffer.at[pl.ds(width, width)], buffer.at[pl.ds(count + width, width)],
                       halo_send.at[2 * i + 1], halo_recv.at[2 * i + 1], down),
            )
        )

    has_above, has_below = sub < SUBS - 1, sub > 0

    def send_halo(which, way):
        pl.when((has_above, has_below)[way])(halos[which][way].start)

    def halo_sent(which, way):
        pl.when((has_above, has_below)[way])(halos[which][way].wait_send)

    def halo_arrived(which, way):
        pl.when((has_below, has_above)[way])(halos[which][way].wait_recv)

    def step_copy(tree, i):
        name, n, low, width, z_first = TREES[tree]
        buffer = {"g2": g2, "g35": g35}[name]
        _, first, second, part, dim, way = STEPS[i]
        offset = (second, first) if z_first else (first, second)
        move = (way, 0) if (dim == 1) == z_first else (0, way)
        half = width // 2
        skip, rows = ((0, width), (0, half), (half, width - half))[part]
        block = buffer.at[pl.ds(at(*offset) * n + low + skip, rows)]
        return remote(block, block, tree_send.at[tree * N_STEPS + i],
                      tree_recv.at[tree * N_STEPS + i], (grp, at(*move)))

    copies = [[step_copy(tree, i) for i in range(N_STEPS)] for tree in range(len(TREES))]

    def begin(tree):
        for i in range(4):
            copies[tree][i].start()

    def arrived(tree, i):
        copies[tree][i].wait_recv()
        for j in range(N_STEPS):
            if STEPS[j][0] == i:
                copies[tree][j].start()

    def root_block(first, count, pick, device):
        block = roots.at[pl.ds(first, count)]
        return remote(block, block, root_send.at[pick], root_recv.at[pick], device)

    def group_block(g, pick, device, first=0, count=SUBS):
        return root_block(g * SUBS + first, count, pick, device)

    ahead, behind = (along_x(1), sub), (along_x(XS - 1), sub)
    half_group = SUBS // 2
    roots_first = [
        root_block(mine, 1, i - 1, (grp, at((1 - core) * i, core * i))) for i in range(1, SIDE)
    ]
    roots_second = [
        root_block(
            grp * SUBS + at((j - y) * (1 - core), (j - z) * core), 1, i * SIDE - 1 + j,
            (grp, at(core * i, (1 - core) * i)),
        )
        for i in range(1, SIDE)
        for j in range(SIDE)
    ]
    roots_x = [group_block(grp, 15, ahead), group_block(grp, 16, behind)]
    roots_far = [
        group_block(along_x(XS - 1), 17, ahead, 0, half_group),
        group_block(along_x(1), 18, behind, half_group, half_group),
    ]
    roots_core = [group_block(along_x(i), 19 + i, (other_core, sub)) for i in range(XS)]

    def after(waited, started):
        for copy in waited:
            copy.wait_recv()
        for copy in started:
            copy.start()


    def relayout_e(k, carry):
        slab = jnp.concatenate([tr[k], tr[k + 32]], axis=0).astype(F32)
        e32[pl.ds(k, 126, stride=E_STRIDE), :] = slab.T
        return carry

    def transfer(t, count):
        parts = []
        for c in range(count):
            rows = e32[pl.ds(pl.multiple_of((t + c) * E_STRIDE, 8), 32), :].astype(BF16)
            parts += [rows[:, :64], rows[:, 64:]]
        return jnp.concatenate(parts, axis=0)

    loads[0].wait()
    lax.fori_loop(0, 32, relayout_e, 0, unroll=4)
    loads[1].wait()
    loads[2].wait()

    lane = lax.broadcasted_iota(jnp.int32, (1, 128), 1)

    def leaf(l, carry):
        live = (lane < cnt[0, l]).astype(F32).astype(BF16)
        m = cur[:, pl.ds(pl.multiple_of(l * 128, 128), 128)] * live
        xm[NEAR_REACH + l] = m
        c = lax.dot_general(bas[l], m, NT, preferred_element_type=F32)
        x0[REACH + l] = c.astype(BF16)
        return carry

    def lift(level, src, src_at, dst, dst_at, low, count, unroll):
        start, _ = span(level - 1)

        def parent(i, carry):
            p = low + i
            pair = src[pl.ds(src_at + 2 * p, 2)].reshape(128, 128)
            c = lax.dot_general(transfer(start + 2 * p, 2), pair, TN, preferred_element_type=F32)
            dst[dst_at + p] = c.astype(BF16)
            return carry

        lax.fori_loop(0, count, parent, 0, unroll=unroll)

    slot2, slot35 = sub * 16, sub * 14
    for h in range(2):
        lax.fori_loop(32 * h, 32 * (h + 1), leaf, 0, unroll=8)
        if h == 0:
            pl.semaphore_wait(barrier, SUBS - 1 + XS - 1 + 1)
        send_halo(0, 1 - h)
        send_halo(1, 1 - h)
        lift(1, x0, REACH, x1, REACH, 16 * h, 16, 8)
        send_halo(2, 1 - h)
        lift(2, x1, REACH, g2, slot2, 8 * h, 8, 8)
        begin(h)
    lift(3, g2, slot2, g35, slot35, 0, 8, 8)
    begin(2)
    lift(4, g35, slot35, g35, slot35 + 8, 0, 4, 4)
    lift(5, g35, slot35 + 8, g35, slot35 + 12, 0, 2, 2)
    begin(3)
    start6, _ = span(LEVELS - 1)
    pair = g35[pl.ds(slot35 + 12, 2)].reshape(128, 128)
    root = lax.dot_general(transfer(start6, 2), pair, TN, preferred_element_type=F32)
    roots[mine] = root.astype(BF16)
    for copy in roots_first:
        copy.start()


    def relayout_c(low, high):
        def one(a, carry):
            for qp in range(3):
                slab = cin[pl.ds(2 * qp, 2), a].reshape(128, 127).astype(F32)
                c32[pl.ds(qp * C_ROWS + a, 127, stride=C_STRIDE), :] = slab.T
            return carry

        lax.fori_loop(low, high, one, 0, unroll=2)

    def couple(level, buffer, place, low, count, unroll):
        start, _ = span(level)
        last = buffer.shape[0] - 1

        def source(q, t):
            return buffer[jnp.clip(place(far[q, t]), 0, last)]

        def target(i, carry):
            t = start + low + i
            matrix = jnp.concatenate(
                [
                    c32[pl.ds(pl.multiple_of(qp * C_ROWS + t * C_STRIDE, 8), 64), :].astype(BF16)
                    for qp in range(3)
                ],
                axis=1,
            )
            stacked = jnp.concatenate([source(q, t) for q in range(6)], axis=0)
            got = jnp.dot(matrix, stacked, preferred_element_type=F32)
            if level == 2:
                d2_out[low + i] = (fields[t] + got).astype(BF16)
            else:
                fields[t] = got
            return carry

        lax.fori_loop(0, count, target, 0, unroll=unroll)

    def join(low, count):
        def one(i, carry):
            p = low + i
            pair = []
            for c in range(2):
                l = 2 * p + c
                got = lax.dot_general(transfer(l, 1), bas[l], TN, preferred_element_type=F32)
                pair.append(got.astype(BF16))
                joined[l] = pair[-1]
            got = lax.dot_general(
                transfer(64 + p, 1), jnp.concatenate(pair, axis=1), TN,
                preferred_element_type=F32,
            ).astype(BF16)
            joined2[2 * p] = got[:, :128]
            joined2[2 * p + 1] = got[:, 128:]
            return carry

        lax.fori_loop(0, count, one, 0, unroll=4)

    near_base = mine * 64 - NEAR_REACH
    outs = []

    def near_field(low, count):
        def one(i, carry):
            t = low + i
            both = jnp.concatenate([fields[t], fields[64 + t // 2]], axis=0).astype(BF16)
            total = lax.dot_general(
                both, jnp.concatenate([bas[t], joined[t]], axis=0), TN,
                preferred_element_type=F32,
            )
            rows = jnp.concatenate(
                [
                    xm[jnp.clip(near[q, t] - near_base, 0, 64 + 2 * NEAR_REACH - 1)]
                    for q in range(5)
                ],
                axis=1,
            )
            blocks = jnp.concatenate([tiles[t, q] for q in range(5)], axis=1)
            total = total + lax.dot_general(rows, blocks, NT, preferred_element_type=F32)
            partial[t] = total.astype(BF16)
            return carry

        lax.fori_loop(0, count, one, 0, unroll=4)
        block = pl.ds(low, count)
        copy = pltpu.make_async_copy(
            partial.at[block], partial_out.at[block], out_sem.at[1 + low // count]
        )
        copy.start()
        outs.append(copy)

    place0 = lambda s: s - (mine * 64 - REACH)
    place1 = lambda s: s - (mine * 32 - REACH)

    def place35(level, offset):
        _, count = span(level)

        def place(s):
            relative = s - grp * SUBS * count
            return (relative // count) * 14 + offset + relative % count

        return place

    def coarse_fields():
        couple(6, roots, lambda s: s, 0, 1, 1)
        couple(5, g35, place35(5, 12), 0, 2, 2)
        couple(4, g35, place35(4, 8), 0, 4, 4)
        couple(3, g35, place35(3, 0), 0, 8, 8)
        d[126] = fields[126].astype(BF16)
        for level in range(LEVELS - 1, 1, -1):
            start, _ = span(level)
            parents, count = span(level + 1)

            def parent(p, carry, start=start, parents=parents, level=level):
                got = jnp.dot(
                    transfer(start + 2 * p, 2), d[parents + p], preferred_element_type=F32
                )
                children = pl.ds(start + 2 * p, 2)
                if level == 2:
                    fields[children] = got.reshape(2, 64, 128)
                else:
                    got = got + fields[children].reshape(128, 128)
                    d[children] = got.reshape(2, 64, 128).astype(BF16)
                return carry

            lax.fori_loop(0, count, parent, 0, unroll=count)

    def beside(kind, i):
        if i == 0:
            if kind == "r":
                loads[3].wait()
            if kind == "n":
                loads[4].wait()
            if kind in HALO_OF:
                for way in range(2):
                    halo_arrived(HALO_OF[kind], way)
        if kind == "r":
            relayout_c(16 * i, 16 * (i + 1))
        elif kind == "c0":
            couple(0, x0, place0, 16 * i, 16, 8)
        elif kind == "c1":
            couple(1, x1, place1, 16 * i, 16, 8)
        elif kind == "j":
            join(8 * i, 8)
            if i == 3:
                copy = pltpu.make_async_copy(joined2, joined_out, out_sem.at[0])
                copy.start()
                outs.append(copy)
        else:
            near_field(8 * i, 8)

    for op in SCHEDULE:
        kind = op[0]
        if kind == "w":
            arrived(op[1], op[2])
        elif kind == "rz":
            after(roots_first, roots_second)
        elif kind == "ry":
            after(roots_second, roots_x + roots_core[:1])
        elif kind == "rx":
            after(roots_x, roots_far + roots_core[1::2])
        elif kind == "rf":
            after(roots_far, roots_core[2:3])
        elif kind == "rc":
            after(roots_core, [])
        elif kind == "f":
            coarse_fields()
        else:
            beside(kind, op[1])

    couple(2, g2, lambda s: s - grp * SUBS * 16, 0, 16, 16)

    for which in range(len(halos)):
        for way in range(2):
            halo_sent(which, way)
    for tree in copies:
        for copy in tree:
            copy.wait_send()
    for copy in roots_first + roots_second + roots_x + roots_far + roots_core:
        copy.wait_send()
    for copy in outs:
        copy.wait()


def main_pass(cnt, currents, basis, tr, matrices, near_tiles, far, near):
    vm = pl.BlockSpec(memory_space=pltpu.VMEM)
    hbm = pl.BlockSpec(memory_space=pl.ANY)
    sm = pl.BlockSpec(memory_space=pltpu.SMEM)
    dma = pltpu.SemaphoreType.DMA
    steps = len(TREES) * N_STEPS
    return pl.pallas_call(
        main_kernel,
        out_shape=(
            jax.ShapeDtypeStruct((64, 128, 128), BF16),
            jax.ShapeDtypeStruct((64, 64, 128), BF16),
            jax.ShapeDtypeStruct((16, 64, 128), BF16),
        ),
        in_specs=[sm, hbm, hbm, hbm, hbm, hbm, sm, sm],
        out_specs=(hbm, hbm, vm),
        scratch_shapes=[
            pltpu.VMEM((128, 8192), BF16),
            pltpu.VMEM((64, 64, 128), BF16),
            pltpu.VMEM((64, 64, 126), BF16),
            pltpu.VMEM((126 * E_STRIDE, 128), F32),
            pltpu.VMEM((64 + 2 * NEAR_REACH, 128, 128), BF16),
            pltpu.VMEM((64 + 2 * REACH, 64, 128), BF16),
            pltpu.VMEM((32 + 2 * REACH, 64, 128), BF16),
            pltpu.VMEM((256, 64, 128), BF16),
            pltpu.VMEM((224, 64, 128), BF16),
            pltpu.VMEM((128, 64, 128), BF16),
            pltpu.VMEM((6, 64, 64, 127), BF16),
            pltpu.VMEM((3 * C_ROWS, 128), F32),
            pltpu.VMEM((64, 5, 128, 128), BF16),
            pltpu.VMEM((127, 64, 128), F32),
            pltpu.VMEM((64, 128, 128), BF16),
            pltpu.VMEM((64, 64, 128), BF16),
            pltpu.VMEM((64, 64, 128), BF16),
            pltpu.VMEM((127, 64, 128), BF16),
            dma((5,)), dma((1 + CHUNKS,)),
            dma((6,)), dma((6,)),
            dma((steps,)), dma((steps,)),
            dma((19 + XS,)), dma((19 + XS,)),
        ],
        compiler_params=pltpu.CompilerParams(
            collective_id=0, has_side_effects=True, vmem_limit_bytes=VMEM_LIMIT
        ),
        name="main_pass",
    )(cnt, currents, basis, tr, matrices, near_tiles, far, near)


BLOCK = 32


def last_kernel(cnt, d2, joined, partial, out):
    g = pl.program_id(0)
    lane = lax.broadcasted_iota(jnp.int32, (1, 128), 1)
    for i in range(BLOCK):
        smooth = lax.dot_general(d2[i // 4], joined[i], TN, preferred_element_type=F32)
        live = (lane < cnt[0, g * BLOCK + i]).astype(F32)
        out[:, i * 128 : (i + 1) * 128] = (smooth + partial[i].astype(F32)) * live


def last_pass(cnt, d2, joined, partial):
    return pl.pallas_call(
        last_kernel,
        grid=(64 // BLOCK,),
        out_shape=jax.ShapeDtypeStruct((128, 8192), F32),
        in_specs=[
            pl.BlockSpec(memory_space=pltpu.SMEM),
            pl.BlockSpec((BLOCK // 4, 64, 128), lambda g: (g, 0, 0)),
            pl.BlockSpec((BLOCK, 64, 128), lambda g: (g, 0, 0)),
            pl.BlockSpec((BLOCK, 128, 128), lambda g: (g, 0, 0)),
        ],
        out_specs=pl.BlockSpec((128, BLOCK * 128), lambda g: (0, g)),
        compiler_params=pltpu.CompilerParams(vmem_limit_bytes=VMEM_LIMIT),
        name="last_pass",
    )(cnt, d2, joined, partial)


def body(
    currents,
    leaf_segment_count,
    leaf_basis,
    transfers,
    coupling,
    far_sources,
    near_tiles,
    near_sources,
):
    basis = jnp.transpose(leaf_basis, (0, 2, 1))
    tr = jnp.transpose(transfers, (1, 2, 0))
    matrices = jnp.transpose(coupling, (1, 2, 3, 0))
    far = jnp.transpose(far_sources, (1, 0))
    near = jnp.transpose(near_sources, (1, 0))
    partial, joined, d2 = main_pass(
        leaf_segment_count, currents, basis, tr, matrices, near_tiles, far, near
    )
    return last_pass(leaf_segment_count, d2, joined, partial)


def solution(mesh):
    return jax.shard_map(
        body,
        mesh=mesh,
        in_specs=(
            P(None, ("grp", "sub")),
            P(("grp", "sub"), None),
            P(("grp", "sub"), None, None),
            P(("grp", "sub"), None, None),
            P(("grp", "sub"), None, None, None),
            P(("grp", "sub"), None),
            P(("grp", "sub"), None, None, None),
            P(("grp", "sub"), None),
        ),
        out_specs=P(None, ("grp", "sub")),
        check_vma=False,
    )
```

```python
import functools

import jax
import jax.numpy as jnp
from jax import lax
from jax.experimental import pallas as pl
from jax.experimental.pallas import tpu as pltpu
from jax.sharding import PartitionSpec as P

LEVELS = 6
REACH = 8
NEAR_REACH = 2
SIDE = 4
SUBS = 16
XS = 4
F32 = jnp.float32
BF16 = jnp.bfloat16
VMEM_LIMIT = 60 * 1024 * 1024

C_STRIDE = 72
C_ROWS = 127 * C_STRIDE
E_STRIDE = 40
NT = (((1,), (1,)), ((), ()))
TN = (((0,), (0,)), ((), ()))


def span(level):
    count = 64 >> level
    return 128 - 2 * count, count


STEPS = (
    (None, 0, 0, 0, 0, 1),
    (None, 0, 0, 0, 0, -1),
    (None, 0, 0, 0, 1, 1),
    (None, 0, 0, 0, 1, -1),
    (0, -1, 0, 1, 0, 1),
    (0, -1, 0, 0, 1, 1),
    (0, -1, 0, 0, 1, -1),
    (1, 1, 0, 2, 0, -1),
    (1, 1, 0, 0, 1, 1),
    (1, 1, 0, 0, 1, -1),
    (2, 0, -1, 1, 1, 1),
    (3, 0, 1, 2, 1, -1),
    (4, 2, 0, 1, 1, 1),
    (4, 2, 0, 1, 1, -1),
    (7, 2, 0, 2, 1, 1),
    (7, 2, 0, 2, 1, -1),
    (8, 1, -1, 0, 1, 1),
    (6, -1, 1, 0, 1, -1),
    (12, 2, -1, 1, 1, 1),
    (15, 2, 1, 2, 1, -1),
)
N_STEPS = len(STEPS)

TREES = (
    ("g2", 16, 0, 8, True),
    ("g2", 16, 8, 8, False),
    ("g35", 14, 0, 7, True),
    ("g35", 14, 7, 7, False),
)
CHUNKS = 8


SCHEDULE = (
    ("r", 0), ("w", 0, 0), ("w", 0, 1), ("w", 0, 2), ("w", 0, 3), ("r", 1), ("w", 1, 0),
    ("w", 1, 1), ("w", 1, 2), ("w", 1, 3), ("r", 2), ("w", 2, 0), ("w", 2, 1), ("w", 2, 2),
    ("w", 2, 3), ("r", 3), ("w", 3, 0), ("w", 3, 1), ("w", 3, 2), ("w", 3, 3), ("rz",), ("j", 0),
    ("j", 1), ("w", 0, 4), ("w", 0, 7), ("w", 0, 8), ("w", 0, 6), ("j", 2), ("j", 3), ("c0", 0),
    ("c0", 1), ("w", 1, 4), ("w", 1, 7), ("w", 1, 8), ("w", 1, 6), ("c0", 2), ("c0", 3),
    ("w", 2, 4), ("w", 2, 7), ("w", 2, 8), ("w", 2, 6), ("c1", 0), ("c1", 1), ("n", 0),
    ("w", 3, 4), ("w", 3, 7), ("w", 3, 8), ("w", 3, 6), ("ry",), ("n", 1), ("n", 2), ("n", 3),
    ("w", 0, 12), ("w", 0, 15), ("n", 4), ("n", 5), ("w", 1, 12), ("w", 1, 15), ("n", 6),
    ("n", 7), ("w", 2, 12), ("w", 2, 15), ("rx",), ("w", 3, 12), ("w", 3, 15), ("rf",), ("rc",),
    ("w", 2, 5), ("w", 2, 9), ("w", 2, 10), ("w", 2, 11), ("w", 2, 13), ("w", 2, 14),
    ("w", 2, 16), ("w", 2, 17), ("w", 2, 18), ("w", 2, 19), ("w", 3, 5), ("w", 3, 9),
    ("w", 3, 10), ("w", 3, 11), ("w", 3, 13), ("w", 3, 14), ("w", 3, 16), ("w", 3, 17),
    ("w", 3, 18), ("w", 3, 19), ("f",), ("w", 0, 5), ("w", 0, 9), ("w", 0, 10), ("w", 0, 11),
    ("w", 0, 13), ("w", 0, 14), ("w", 0, 16), ("w", 0, 17), ("w", 0, 18), ("w", 0, 19),
    ("w", 1, 5), ("w", 1, 9), ("w", 1, 10), ("w", 1, 11), ("w", 1, 13), ("w", 1, 14),
    ("w", 1, 16), ("w", 1, 17), ("w", 1, 18), ("w", 1, 19),
)
HALO_OF = {"n": 0, "c0": 1, "c1": 2}


def main_kernel(
    cnt, currents, basis, transfers, coupling, near_tiles, far, near,
    partial_out, joined_out, d2_out,
    cur, bas, tr, e32, xm, x0, x1, g2, g35, roots, cin, c32, tiles, fields, partial, joined, joined2, d,
    in_sem, out_sem, halo_send, halo_recv, tree_send, tree_recv,
    root_send, root_recv,
):
    grp = lax.axis_index("grp")
    sub = lax.axis_index("sub")
    y = sub // SIDE
    z = sub % SIDE
    core = grp % 2
    x = grp // 2
    mine = grp * SUBS + sub

    def at(dy, dz):
        return ((y + dy + SIDE) % SIDE) * SIDE + (z + dz + SIDE) % SIDE

    def along_x(i):
        return ((x + i) % XS) * 2 + core

    other_core = x * 2 + (1 - core)

    loads = [
        pltpu.make_async_copy(src, dst, in_sem.at[i])
        for i, (src, dst) in enumerate(
            ((transfers, tr), (currents, cur), (basis, bas), (coupling, cin), (near_tiles, tiles))
        )
    ]
    for copy in loads:
        copy.start()

    barrier = pltpu.get_barrier_semaphore()

    def greet(device):
        pl.semaphore_signal(
            barrier, inc=1, device_id=device, device_id_type=pl.DeviceIdType.MESH
        )

    for i in range(1, SUBS):
        greet((grp, (sub + i) % SUBS))
    for i in range(1, XS):
        greet((along_x(i), sub))
    greet((other_core, sub))

    def remote(src, dst, send, recv, device):
        return pltpu.make_async_remote_copy(
            src_ref=src, dst_ref=dst, send_sem=send, recv_sem=recv,
            device_id=device, device_id_type=pl.DeviceIdType.MESH,
        )

    up, down = (grp, (sub + 1) % SUBS), (grp, (sub + SUBS - 1) % SUBS)
    halos = []
    for i, (buffer, width, count) in enumerate(
        ((xm, NEAR_REACH, 64), (x0, REACH, 64), (x1, REACH, 32))
    ):
        halos.append(
            (
                remote(buffer.at[pl.ds(count, width)], buffer.at[pl.ds(0, width)],
                       halo_send.at[2 * i], halo_recv.at[2 * i], up),
                remote(buffer.at[pl.ds(width, width)], buffer.at[pl.ds(count + width, width)],
                       halo_send.at[2 * i + 1], halo_recv.at[2 * i + 1], down),
            )
        )

    has_above, has_below = sub < SUBS - 1, sub > 0

    def send_halo(which, way):
        pl.when((has_above, has_below)[way])(halos[which][way].start)

    def halo_sent(which, way):
        pl.when((has_above, has_below)[way])(halos[which][way].wait_send)

    def halo_arrived(which, way):
        pl.when((has_below, has_above)[way])(halos[which][way].wait_recv)

    def step_copy(tree, i):
        name, n, low, width, z_first = TREES[tree]
        buffer = {"g2": g2, "g35": g35}[name]
        _, first, second, part, dim, way = STEPS[i]
        offset = (second, first) if z_first else (first, second)
        move = (way, 0) if (dim == 1) == z_first else (0, way)
        half = width // 2
        skip, rows = ((0, width), (0, half), (half, width - half))[part]
        block = buffer.at[pl.ds(at(*offset) * n + low + skip, rows)]
        return remote(block, block, tree_send.at[tree * N_STEPS + i],
                      tree_recv.at[tree * N_STEPS + i], (grp, at(*move)))

    copies = [[step_copy(tree, i) for i in range(N_STEPS)] for tree in range(len(TREES))]

    def begin(tree):
        for i in range(4):
            copies[tree][i].start()

    def arrived(tree, i):
        copies[tree][i].wait_recv()
        for j in range(N_STEPS):
            if STEPS[j][0] == i:
                copies[tree][j].start()

    def root_block(first, count, pick, device):
        block = roots.at[pl.ds(first, count)]
        return remote(block, block, root_send.at[pick], root_recv.at[pick], device)

    def group_block(g, pick, device, first=0, count=SUBS):
        return root_block(g * SUBS + first, count, pick, device)

    ahead, behind = (along_x(1), sub), (along_x(XS - 1), sub)
    half_group = SUBS // 2
    roots_first = [
        root_block(mine, 1, i - 1, (grp, at((1 - core) * i, core * i))) for i in range(1, SIDE)
    ]
    roots_second = [
        root_block(
            grp * SUBS + at((j - y) * (1 - core), (j - z) * core), 1, i * SIDE - 1 + j,
            (grp, at(core * i, (1 - core) * i)),
        )
        for i in range(1, SIDE)
        for j in range(SIDE)
    ]
    roots_x = [group_block(grp, 15, ahead), group_block(grp, 16, behind)]
    roots_far = [
        group_block(along_x(XS - 1), 17, ahead, 0, half_group),
        group_block(along_x(1), 18, behind, half_group, half_group),
    ]
    roots_core = [group_block(along_x(i), 19 + i, (other_core, sub)) for i in range(XS)]

    def after(waited, started):
        for copy in waited:
            copy.wait_recv()
        for copy in started:
            copy.start()


    def relayout_e(k, carry):
        slab = jnp.concatenate([tr[k], tr[k + 32]], axis=0).astype(F32)
        e32[pl.ds(k, 126, stride=E_STRIDE), :] = slab.T
        return carry

    def transfer(t, count):
        parts = []
        for c in range(count):
            rows = e32[pl.ds(pl.multiple_of((t + c) * E_STRIDE, 8), 32), :].astype(BF16)
            parts += [rows[:, :64], rows[:, 64:]]
        return jnp.concatenate(parts, axis=0)

    loads[0].wait()
    lax.fori_loop(0, 32, relayout_e, 0, unroll=4)
    loads[1].wait()
    loads[2].wait()

    lane = lax.broadcasted_iota(jnp.int32, (1, 128), 1)

    def leaf(l, carry):
        live = (lane < cnt[0, l]).astype(F32).astype(BF16)
        m = cur[:, pl.ds(pl.multiple_of(l * 128, 128), 128)] * live
        xm[NEAR_REACH + l] = m
        c = lax.dot_general(bas[l], m, NT, preferred_element_type=F32)
        x0[REACH + l] = c.astype(BF16)
        return carry

    def lift(level, src, src_at, dst, dst_at, low, count, unroll):
        start, _ = span(level - 1)

        def parent(i, carry):
            p = low + i
            pair = src[pl.ds(src_at + 2 * p, 2)].reshape(128, 128)
            c = lax.dot_general(transfer(start + 2 * p, 2), pair, TN, preferred_element_type=F32)
            dst[dst_at + p] = c.astype(BF16)
            return carry

        lax.fori_loop(0, count, parent, 0, unroll=unroll)

    slot2, slot35 = sub * 16, sub * 14
    for h in range(2):
        lax.fori_loop(32 * h, 32 * (h + 1), leaf, 0, unroll=8)
        if h == 0:
            pl.semaphore_wait(barrier, SUBS - 1 + XS - 1 + 1)
        send_halo(0, 1 - h)
        lift(1, x0, REACH, x1, REACH, 16 * h, 16, 8)
        lift(2, x1, REACH, g2, slot2, 8 * h, 8, 8)
        begin(h)
    lift(3, g2, slot2, g35, slot35, 0, 8, 8)
    begin(2)
    lift(4, g35, slot35, g35, slot35 + 8, 0, 4, 4)
    lift(5, g35, slot35 + 8, g35, slot35 + 12, 0, 2, 2)
    begin(3)
    start6, _ = span(LEVELS - 1)
    pair = g35[pl.ds(slot35 + 12, 2)].reshape(128, 128)
    root = lax.dot_general(transfer(start6, 2), pair, TN, preferred_element_type=F32)
    roots[mine] = root.astype(BF16)
    for copy in roots_first:
        copy.start()
    for which in (1, 2):
        for way in range(2):
            send_halo(which, way)


    def relayout_c(low, high):
        def one(a, carry):
            for qp in range(3):
                slab = cin[pl.ds(2 * qp, 2), a].reshape(128, 127).astype(F32)
                c32[pl.ds(qp * C_ROWS + a, 127, stride=C_STRIDE), :] = slab.T
            return carry

        lax.fori_loop(low, high, one, 0, unroll=2)

    def couple(level, buffer, place, low, count, unroll):
        start, _ = span(level)
        last = buffer.shape[0] - 1

        def source(q, t):
            return buffer[jnp.clip(place(far[q, t]), 0, last)]

        def target(i, carry):
            t = start + low + i
            matrix = jnp.concatenate(
                [
                    c32[pl.ds(pl.multiple_of(qp * C_ROWS + t * C_STRIDE, 8), 64), :].astype(BF16)
                    for qp in range(3)
                ],
                axis=1,
            )
            stacked = jnp.concatenate([source(q, t) for q in range(6)], axis=0)
            got = jnp.dot(matrix, stacked, preferred_element_type=F32)
            if level == 2:
                d2_out[low + i] = (fields[t] + got).astype(BF16)
            else:
                fields[t] = got
            return carry

        lax.fori_loop(0, count, target, 0, unroll=unroll)

    def join(low, count):
        def one(i, carry):
            p = low + i
            pair = []
            for c in range(2):
                l = 2 * p + c
                got = lax.dot_general(transfer(l, 1), bas[l], TN, preferred_element_type=F32)
                pair.append(got.astype(BF16))
                joined[l] = pair[-1]
            got = lax.dot_general(
                transfer(64 + p, 1), jnp.concatenate(pair, axis=1), TN,
                preferred_element_type=F32,
            ).astype(BF16)
            joined2[2 * p] = got[:, :128]
            joined2[2 * p + 1] = got[:, 128:]
            return carry

        lax.fori_loop(0, count, one, 0, unroll=4)

    near_base = mine * 64 - NEAR_REACH
    outs = []

    def near_field(low, count):
        def one(i, carry):
            t = low + i
            both = jnp.concatenate([fields[t], fields[64 + t // 2]], axis=0).astype(BF16)
            total = lax.dot_general(
                both, jnp.concatenate([bas[t], joined[t]], axis=0), TN,
                preferred_element_type=F32,
            )
            rows = jnp.concatenate(
                [
                    xm[jnp.clip(near[q, t] - near_base, 0, 64 + 2 * NEAR_REACH - 1)]
                    for q in range(5)
                ],
                axis=1,
            )
            blocks = jnp.concatenate([tiles[t, q] for q in range(5)], axis=1)
            total = total + lax.dot_general(rows, blocks, NT, preferred_element_type=F32)
            partial[t] = total.astype(BF16)
            return carry

        lax.fori_loop(0, count, one, 0, unroll=4)
        block = pl.ds(low, count)
        copy = pltpu.make_async_copy(
            partial.at[block], partial_out.at[block], out_sem.at[1 + low // count]
        )
        copy.start()
        outs.append(copy)

    place0 = lambda s: s - (mine * 64 - REACH)
    place1 = lambda s: s - (mine * 32 - REACH)

    def place35(level, offset):
        _, count = span(level)

        def place(s):
            relative = s - grp * SUBS * count
            return (relative // count) * 14 + offset + relative % count

        return place

    def coarse_fields():
        couple(6, roots, lambda s: s, 0, 1, 1)
        couple(5, g35, place35(5, 12), 0, 2, 2)
        couple(4, g35, place35(4, 8), 0, 4, 4)
        couple(3, g35, place35(3, 0), 0, 8, 8)
        d[126] = fields[126].astype(BF16)
        for level in range(LEVELS - 1, 1, -1):
            start, _ = span(level)
            parents, count = span(level + 1)

            def parent(p, carry, start=start, parents=parents, level=level):
                got = jnp.dot(
                    transfer(start + 2 * p, 2), d[parents + p], preferred_element_type=F32
                )
                children = pl.ds(start + 2 * p, 2)
                if level == 2:
                    fields[children] = got.reshape(2, 64, 128)
                else:
                    got = got + fields[children].reshape(128, 128)
                    d[children] = got.reshape(2, 64, 128).astype(BF16)
                return carry

            lax.fori_loop(0, count, parent, 0, unroll=count)

    def beside(kind, i):
        if i == 0:
            if kind == "r":
                loads[3].wait()
            if kind == "n":
                loads[4].wait()
            if kind in HALO_OF:
                for way in range(2):
                    halo_arrived(HALO_OF[kind], way)
        if kind == "r":
            relayout_c(16 * i, 16 * (i + 1))
        elif kind == "c0":
            couple(0, x0, place0, 16 * i, 16, 8)
        elif kind == "c1":
            couple(1, x1, place1, 16 * i, 16, 8)
        elif kind == "j":
            join(8 * i, 8)
            if i == 3:
                copy = pltpu.make_async_copy(joined2, joined_out, out_sem.at[0])
                copy.start()
                outs.append(copy)
        else:
            near_field(8 * i, 8)

    for op in SCHEDULE:
        kind = op[0]
        if kind == "w":
            arrived(op[1], op[2])
        elif kind == "rz":
            after(roots_first, roots_second)
        elif kind == "ry":
            after(roots_second, roots_x + roots_core[:1])
        elif kind == "rx":
            after(roots_x, roots_far + roots_core[1::2])
        elif kind == "rf":
            after(roots_far, roots_core[2:3])
        elif kind == "rc":
            after(roots_core, [])
        elif kind == "f":
            coarse_fields()
        else:
            beside(kind, op[1])

    couple(2, g2, lambda s: s - grp * SUBS * 16, 0, 16, 16)

    for which in range(len(halos)):
        for way in range(2):
            halo_sent(which, way)
    for tree in copies:
        for copy in tree:
            copy.wait_send()
    for copy in roots_first + roots_second + roots_x + roots_far + roots_core:
        copy.wait_send()
    for copy in outs:
        copy.wait()


def main_pass(cnt, currents, basis, tr, matrices, near_tiles, far, near):
    vm = pl.BlockSpec(memory_space=pltpu.VMEM)
    hbm = pl.BlockSpec(memory_space=pl.ANY)
    sm = pl.BlockSpec(memory_space=pltpu.SMEM)
    dma = pltpu.SemaphoreType.DMA
    steps = len(TREES) * N_STEPS
    return pl.pallas_call(
        main_kernel,
        out_shape=(
            jax.ShapeDtypeStruct((64, 128, 128), BF16),
            jax.ShapeDtypeStruct((64, 64, 128), BF16),
            jax.ShapeDtypeStruct((16, 64, 128), BF16),
        ),
        in_specs=[sm, hbm, hbm, hbm, hbm, hbm, sm, sm],
        out_specs=(hbm, hbm, vm),
        scratch_shapes=[
            pltpu.VMEM((128, 8192), BF16),
            pltpu.VMEM((64, 64, 128), BF16),
            pltpu.VMEM((64, 64, 126), BF16),
            pltpu.VMEM((126 * E_STRIDE, 128), F32),
            pltpu.VMEM((64 + 2 * NEAR_REACH, 128, 128), BF16),
            pltpu.VMEM((64 + 2 * REACH, 64, 128), BF16),
            pltpu.VMEM((32 + 2 * REACH, 64, 128), BF16),
            pltpu.VMEM((256, 64, 128), BF16),
            pltpu.VMEM((224, 64, 128), BF16),
            pltpu.VMEM((128, 64, 128), BF16),
            pltpu.VMEM((6, 64, 64, 127), BF16),
            pltpu.VMEM((3 * C_ROWS, 128), F32),
            pltpu.VMEM((64, 5, 128, 128), BF16),
            pltpu.VMEM((127, 64, 128), F32),
            pltpu.VMEM((64, 128, 128), BF16),
            pltpu.VMEM((64, 64, 128), BF16),
            pltpu.VMEM((64, 64, 128), BF16),
            pltpu.VMEM((127, 64, 128), BF16),
            dma((5,)), dma((1 + CHUNKS,)),
            dma((6,)), dma((6,)),
            dma((steps,)), dma((steps,)),
            dma((19 + XS,)), dma((19 + XS,)),
        ],
        compiler_params=pltpu.CompilerParams(
            collective_id=0, has_side_effects=True, vmem_limit_bytes=VMEM_LIMIT
        ),
        name="main_pass",
    )(cnt, currents, basis, tr, matrices, near_tiles, far, near)


BLOCK = 32


def last_kernel(cnt, d2, joined, partial, out):
    g = pl.program_id(0)
    lane = lax.broadcasted_iota(jnp.int32, (1, 128), 1)
    for i in range(BLOCK):
        smooth = lax.dot_general(d2[i // 4], joined[i], TN, preferred_element_type=F32)
        live = (lane < cnt[0, g * BLOCK + i]).astype(F32)
        out[:, i * 128 : (i + 1) * 128] = (smooth + partial[i].astype(F32)) * live


def last_pass(cnt, d2, joined, partial):
    return pl.pallas_call(
        last_kernel,
        grid=(64 // BLOCK,),
        out_shape=jax.ShapeDtypeStruct((128, 8192), F32),
        in_specs=[
            pl.BlockSpec(memory_space=pltpu.SMEM),
            pl.BlockSpec((BLOCK // 4, 64, 128), lambda g: (g, 0, 0)),
            pl.BlockSpec((BLOCK, 64, 128), lambda g: (g, 0, 0)),
            pl.BlockSpec((BLOCK, 128, 128), lambda g: (g, 0, 0)),
        ],
        out_specs=pl.BlockSpec((128, BLOCK * 128), lambda g: (0, g)),
        compiler_params=pltpu.CompilerParams(vmem_limit_bytes=VMEM_LIMIT),
        name="last_pass",
    )(cnt, d2, joined, partial)


def body(
    currents,
    leaf_segment_count,
    leaf_basis,
    transfers,
    coupling,
    far_sources,
    near_tiles,
    near_sources,
):
    basis = jnp.transpose(leaf_basis, (0, 2, 1))
    tr = jnp.transpose(transfers, (1, 2, 0))
    matrices = jnp.transpose(coupling, (1, 2, 3, 0))
    far = jnp.transpose(far_sources, (1, 0))
    near = jnp.transpose(near_sources, (1, 0))
    partial, joined, d2 = main_pass(
        leaf_segment_count, currents, basis, tr, matrices, near_tiles, far, near
    )
    return last_pass(leaf_segment_count, d2, joined, partial)


def solution(mesh):
    return jax.shard_map(
        body,
        mesh=mesh,
        in_specs=(
            P(None, ("grp", "sub")),
            P(("grp", "sub"), None),
            P(("grp", "sub"), None, None),
            P(("grp", "sub"), None, None),
            P(("grp", "sub"), None, None, None),
            P(("grp", "sub"), None),
            P(("grp", "sub"), None, None, None),
            P(("grp", "sub"), None),
        ),
        out_specs=P(None, ("grp", "sub")),
        check_vma=False,
    )
```
